128 devices in a mesh: gx: 4 (over z), gy: 32 (over x, y, core).
Axes of the slice: x: 4, y: 4, z: 4, core: 2. Of those that a mesh axis runs over, the one named last changes fastest.
Arguments:
- gauss_params: float32 [55, 262144], P(None, ('gx', 'gy')), may hold values from -16 to 2064, as said below
- first_moment: float32 [55, 262144], P(None, ('gx', 'gy')), may hold values from -0.3 to 0.3
- second_moment: float32 [55, 262144], P(None, ('gx', 'gy')), may hold values from 0.001 to 0.1
- splat_lists: int32 [2, 2048, 512], P(None, ('gx', 'gy')), may hold values from 0 to 262143, as said below
- tile_ids: int32 [2, 2048], P(None, ('gx', 'gy')), may hold values from 0 to 2047, as said below
- targets: float32 [2, 2048, 3, 256], P(None, ('gx', 'gy')), may hold values from 0 to 1
- camera: float32 [2, 2], replicated, may hold values from -3 to 3
Outputs:
- updated_params: float32 [55, 262144], P(None, ('gx', 'gy'))
- updated_first: float32 [55, 262144], P(None, ('gx', 'gy'))
- updated_second: float32 [55, 262144], P(None, ('gx', 'gy'))
- rendered: float32 [2, 2048, 3, 256], P(None, ('gx', 'gy'))
- loss: float32 [2], replicated
The draws below stay inside these ranges and needn't reach their ends.
Inputs may be any that keep to these rules, and one draw needn't show every extreme that they name: `gauss_params`: rows of each column: x and y (positions scaled by depth), depth z in [1, 2], two log scales, an angle, an opacity logit, then 16 harmonic coefficients for red, green and blue in turn. `splat_lists`: gaussian ids; the Gaussians with ids k * 2048 to (k + 1) * 2048 - 1 belong to device k along gx+gy. In each step, the entries of one device's 16 tile slots name Gaussians of one owner at most 128 times, and some owner is named exactly 128 times by every device. `tile_ids`: image tiles numbered row by row over 64 columns; within a step, slots show distinct tiles while 2048 <= 2048.
All inputs are finite; a program needn't handle non-finite values.
Results may differ from the reference program's by a relative error of at most 0.0014.
Values sent between devices are 32-bit elements; how exact they have to be, the bound alone decides.
A program may use at most 64 MiB of HBM per device.

```python
import math
import jax
import jax.numpy as jnp
from jax import lax

SIDE = 16
PIX = 256
K = 512
NCOEF = 16
PROWS = 55
STEPS = 2
IMG_TX = 64
IMG_TY = 32
NT_IMG = 2048
G_DEV = 2048
OWNERS = 128
GAUSS = 262144
TILES = 2048
S_DEV = 8192
CAP = 128


depth_levels = 4096


def depth_table(base_key):
    return jax.random.randint(jax.random.fold_in(base_key, 7), (GAUSS,), 0, depth_levels, dtype=jnp.int32)


def list_parts(base_key, step_index):
    step_key = jax.random.fold_in(base_key, 1000 + step_index)
    key_perm, key_heavy, key_weight, key_shuffle, key_near, key_copy = jax.random.split(step_key, 6)
    tile_order = jax.random.permutation(key_perm, NT_IMG).astype(jnp.int32)
    tiles_drawn = tile_order[jnp.arange(TILES, dtype=jnp.int32) % NT_IMG]
    heavy_owner = jax.random.randint(key_heavy, (), 0, OWNERS, dtype=jnp.int32)
    owner_range = jnp.arange(OWNERS, dtype=jnp.int32)
    weights = jax.random.randint(key_weight, (OWNERS, OWNERS), 2, 4, dtype=jnp.int32)
    weights = jnp.where(owner_range[None, :] == heavy_owner, 0, weights)
    running = jnp.cumsum(weights, axis=1)
    ends_at = running * (S_DEV - CAP) // running[:, -1:]
    counts = ends_at - jnp.concatenate([jnp.zeros((OWNERS, 1), jnp.int32), ends_at[:, :-1]], 1)
    counts = counts + jnp.where(owner_range[None, :] == heavy_owner, CAP, 0)
    limits = jnp.cumsum(counts, axis=1)
    slot_index = jnp.arange(S_DEV, dtype=jnp.int32)
    sequence = jax.vmap(lambda limit_row: jnp.searchsorted(limit_row, slot_index, side='right'))(limits).astype(jnp.int32)
    shuffles = jax.vmap(lambda shuffle_key: jax.random.permutation(shuffle_key, S_DEV))(jax.random.split(key_shuffle, OWNERS))
    owner_of = jnp.take_along_axis(sequence, shuffles.astype(jnp.int32), axis=1).reshape(TILES, K)
    tile_x = tiles_drawn % IMG_TX
    tile_y = tiles_drawn // IMG_TX
    nearby = jax.random.randint(key_near, (2, TILES, K), -1, 2, dtype=jnp.int32)
    near_x = jnp.clip(tile_x[:, None] + nearby[0], 0, IMG_TX - 1)
    near_y = jnp.clip(tile_y[:, None] + nearby[1], 0, IMG_TY - 1)
    home_tile = near_y * IMG_TX + near_x
    copy_index = jax.random.randint(key_copy, (TILES, K), 0, G_DEV // NT_IMG, dtype=jnp.int32)
    gauss_id = owner_of * G_DEV + copy_index * NT_IMG + home_tile
    depth_key = depth_table(base_key)[gauss_id]
    scores = depth_key * K + jnp.arange(K, dtype=jnp.int32)[None, :]
    order_in = jnp.argsort(scores, axis=1)
    gauss_id = jnp.take_along_axis(gauss_id, order_in, axis=1)
    return (tiles_drawn.astype(jnp.int32), gauss_id.astype(jnp.int32))


def draw_splat_lists(key, part):
    return jnp.stack([list_parts(key, step_index)[1] for step_index in range(STEPS)])


def draw_tile_ids(key, part):
    return jnp.stack([list_parts(key, step_index)[0] for step_index in range(STEPS)])


def draw_gauss_params(key, part):
    index_all = jnp.arange(GAUSS, dtype=jnp.int32)
    home_tile = index_all % G_DEV % NT_IMG
    centre_x = (home_tile % IMG_TX).astype(jnp.float32) * SIDE + 0.5 * SIDE
    centre_y = (home_tile // IMG_TX).astype(jnp.float32) * SIDE + 0.5 * SIDE
    float_keys = jax.random.split(jax.random.fold_in(key, 23), 7)
    depth_z = 1.0 + (depth_table(key).astype(jnp.float32) + jax.random.uniform(float_keys[0], (GAUSS,))) / depth_levels
    jitter = jnp.clip(6.0 * jax.random.normal(float_keys[1], (2, GAUSS)), -16.0, 16.0)
    spread = jnp.exp(jax.random.uniform(float_keys[2], (2, GAUSS), minval=math.log(3.0), maxval=math.log(10.0)))
    logit_value = jax.random.uniform(float_keys[3], (GAUSS,), minval=-3.5, maxval=-1.0)
    coeffs = jnp.clip(0.25 * jax.random.normal(float_keys[5], (3 * NCOEF, GAUSS)), -1.0, 1.0)
    angle_value = jax.random.uniform(float_keys[6], (GAUSS,), minval=-math.pi, maxval=math.pi)
    geometry = jnp.stack([(centre_x + jitter[0]) * depth_z, (centre_y + jitter[1]) * depth_z, depth_z, jnp.log(spread[0] * depth_z), jnp.log(spread[1] * depth_z), angle_value, logit_value])
    return jnp.concatenate([geometry, coeffs], 0).astype(jnp.float32)


def shard_levels(stream_key, extent, pieces, low, top_value):
    gain = 1.0
    for position, parts in pieces:
        steps = jax.random.uniform(jax.random.fold_in(jax.random.fold_in(stream_key, 6), position), (parts,), jnp.float32, low / len(pieces), top_value / len(pieces))
        gain = gain * jnp.repeat(jnp.exp(steps), extent[position] // parts).reshape((-1,) + (1,) * (len(extent) - 1 - position))
    return gain


def normal_values(rng, shape, scale, reach, shards=(), held_as=jnp.bfloat16):
    factor_of = shard_levels(rng, shape, shards, -0.22, 0.18) if shards else 1.0
    result = jax.random.normal(rng, shape, jnp.float32) * scale * factor_of
    return jnp.minimum(jnp.maximum(result, -reach), reach).astype(held_as)


def setup_inputs(seed: int = 0) -> dict:
    streams_of = jax.random.split(jax.random.key(seed), 8)
    return {
        "gauss_params": draw_gauss_params(jax.random.fold_in(streams_of[7], 71), 0),
        "first_moment": normal_values(streams_of[1], (PROWS, GAUSS), 0.05, 0.3, ((1, 128),), jnp.float32),
        "second_moment": jnp.clip(jnp.exp(math.log(0.1) - 4.6051702 * jax.random.uniform(streams_of[2], (PROWS, GAUSS), jnp.float32) ** shard_levels(streams_of[2], (PROWS, GAUSS), ((1, 128),), -0.2, 0.2)), 0.001, 0.1),
        "splat_lists": draw_splat_lists(jax.random.fold_in(streams_of[7], 71), 0),
        "tile_ids": draw_tile_ids(jax.random.fold_in(streams_of[7], 71), 0),
        "targets": jnp.clip(1.0 * jax.random.uniform(streams_of[5], (STEPS, TILES, 3, PIX), jnp.float32) ** shard_levels(streams_of[5], (STEPS, TILES, 3, PIX), ((1, 128),), -0.2, 0.2), 0.0, 1.0),
        "camera": jnp.clip(jax.random.uniform(streams_of[6], (STEPS, 2), jnp.float32, -3.0, 3.0), -3.0, 3.0),
    }


beta_one = 0.9
beta_two = 0.999
adam_eps = 1e-08
learn_rate = 0.01
adam_start = 1000
splat_fields = 9
band_zero = 0.28209479177387814
band_one = 0.4886025119029199
band_two = (1.0925484305920792, -1.0925484305920792, 0.31539156525252005, -1.0925484305920792, 0.5462742152960396)
band_three = (-0.5900435899266435, 2.890611442640554, -0.4570457994644658, 0.3731763325901154, -0.4570457994644658, 1.445305721320277, -0.5900435899266435)

def harmonics(ray_x, ray_y, ray_z):
    sq_x = ray_x * ray_x
    sq_y = ray_y * ray_y
    sq_z = ray_z * ray_z
    return jnp.stack([band_zero * jnp.ones_like(ray_x), -band_one * ray_y, band_one * ray_z, -band_one * ray_x, band_two[0] * ray_x * ray_y, band_two[1] * ray_y * ray_z, band_two[2] * (2.0 * sq_z - sq_x - sq_y), band_two[3] * ray_x * ray_z, band_two[4] * (sq_x - sq_y), band_three[0] * ray_y * (3.0 * sq_x - sq_y), band_three[1] * ray_x * ray_y * ray_z, band_three[2] * ray_y * (4.0 * sq_z - sq_x - sq_y), band_three[3] * ray_z * (2.0 * sq_z - 3.0 * sq_x - 3.0 * sq_y), band_three[4] * ray_x * (4.0 * sq_z - sq_x - sq_y), band_three[5] * ray_z * (sq_x - sq_y), band_three[6] * ray_x * (sq_x - 3.0 * sq_y)])

def project(gauss_rows, camera_row):
    image_width = 1.0 * SIDE * IMG_TX
    image_height = 1.0 * SIDE * IMG_TY
    depth_z = gauss_rows[2]
    screen_u = (gauss_rows[0] - camera_row[0]) / depth_z
    screen_v = (gauss_rows[1] - camera_row[1]) / depth_z
    inv_one = depth_z * depth_z * jnp.exp(-2.0 * gauss_rows[3])
    inv_two = depth_z * depth_z * jnp.exp(-2.0 * gauss_rows[4])
    cosine = jnp.cos(gauss_rows[5])
    sine_angle = jnp.sin(gauss_rows[5])
    conic_a = cosine * cosine * inv_one + sine_angle * sine_angle * inv_two
    conic_b = cosine * sine_angle * (inv_one - inv_two)
    conic_c = sine_angle * sine_angle * inv_one + cosine * cosine * inv_two
    opacity = 0.99 * jax.nn.sigmoid(gauss_rows[6])
    ray_x = (screen_u - 0.5 * image_width) / image_width
    ray_y = (screen_v - 0.5 * image_height) / image_width
    factor = lax.rsqrt(ray_x * ray_x + ray_y * ray_y + 1.0)
    harmonic_basis = harmonics(ray_x * factor, ray_y * factor, factor)
    coeffs = gauss_rows[7:].reshape(3, NCOEF, gauss_rows.shape[1])
    colour = 0.5 + lax.optimization_barrier(jnp.sum(coeffs * harmonic_basis[None], axis=1))
    geometry = jnp.stack([screen_u, screen_v, conic_a, conic_b, conic_c, opacity])
    return jnp.concatenate([geometry, colour], 0)

def pixel_grid(tile_row):
    cell_index = jnp.arange(SIDE * SIDE, dtype=jnp.int32)
    column = (tile_row % IMG_TX)[:, None] * SIDE + cell_index % SIDE
    row_pix = (tile_row // IMG_TX)[:, None] * SIDE + cell_index // SIDE
    return jnp.stack([column, row_pix], 1).astype(jnp.float32) + 0.5

def render(splat_rows, centres):
    delta_x = centres[0][None, :] - splat_rows[0][:, None]
    delta_y = centres[1][None, :] - splat_rows[1][:, None]
    exponent = -0.5 * (splat_rows[2][:, None] * delta_x * delta_x + 2.0 * splat_rows[3][:, None] * delta_x * delta_y + splat_rows[4][:, None] * delta_y * delta_y)
    opaque = splat_rows[5][:, None] * jnp.exp(exponent)
    log_keep = jnp.log1p(-opaque)
    before = jnp.cumsum(log_keep, axis=0) - log_keep
    weight = jnp.exp(before) * opaque
    return jnp.dot(splat_rows[6:9], weight, precision=lax.Precision.HIGHEST, preferred_element_type=jnp.float32)

def tile_terms(splat_rows, centres, target):
    picture, pullback = jax.vjp(lambda values: render(values, centres), splat_rows)
    residual = picture - target
    return (picture, pullback(residual)[0], 0.5 * jnp.sum(residual * residual))

def adam_update(params, moment_one, second, gradient, step_index):
    step_count = adam_start + step_index + 1
    moment_one = beta_one * moment_one + (1.0 - beta_one) * gradient
    second = beta_two * second + (1.0 - beta_two) * gradient * gradient
    scaled_first = moment_one / (1.0 - beta_one ** step_count)
    scaled_second = second / (1.0 - beta_two ** step_count)
    params = params - learn_rate * scaled_first / (jnp.sqrt(scaled_second) + adam_eps)
    return (params, moment_one, second)

def reference(gauss_params, first_moment, second_moment, splat_lists, tile_ids, targets, camera):
    params, moment_one, moment_two = (gauss_params, first_moment, second_moment)
    pictures = []
    losses = []
    for step_index in range(STEPS):
        camera_row = camera[step_index]
        projected, pullback = jax.vjp(lambda values: project(values, camera_row), params)
        listed = splat_lists[step_index].astype(jnp.int32)
        gathered = jnp.moveaxis(projected[:, listed], 1, 0)
        centres = pixel_grid(tile_ids[step_index].astype(jnp.int32))
        picture, slot_grads, halves = lax.map(lambda tile_parts: tile_terms(tile_parts[0], tile_parts[1], tile_parts[2]), (gathered, centres, targets[step_index]))
        flat_grads = jnp.moveaxis(slot_grads, 0, 1).reshape(splat_fields, -1)
        summed = jnp.zeros_like(projected).at[:, listed.reshape(-1)].add(flat_grads)
        gradient = pullback(summed)[0]
        params, moment_one, moment_two = adam_update(params, moment_one, moment_two, gradient, step_index)
        pictures.append(picture)
        losses.append(jnp.sum(halves) / (3.0 * SIDE * SIDE * TILES))
    return (params, moment_one, moment_two, jnp.stack(pictures), jnp.stack(losses))
```

```python
import math

import jax
import jax.numpy as jnp
import numpy as np
from jax import lax
from jax.experimental import pallas as pl
from jax.experimental.pallas import tpu as pltpu
from jax.sharding import PartitionSpec as P

SIDE = 16
PIX = 256
NCOEF = 16
STEPS = 2
IMG_TX = 64
IMG_TY = 32
OWN = 128
LANES = 128
TILES_DEV = 16
LIST = 512
SLABS = LIST * TILES_DEV // 128
FIELDS = 9
F32 = jnp.float32
BF16 = jnp.bfloat16
I32 = jnp.int32

beta_one = 0.9
beta_two = 0.999
adam_eps = 1e-08
learn_rate = 0.01
adam_start = 1000
band_zero = 0.28209479177387814
band_one = 0.4886025119029199
band_two = (
    1.0925484305920792,
    -1.0925484305920792,
    0.31539156525252005,
    -1.0925484305920792,
    0.5462742152960396,
)
band_three = (
    -0.5900435899266435,
    2.890611442640554,
    -0.4570457994644658,
    0.3731763325901154,
    -0.4570457994644658,
    1.445305721320277,
    -0.5900435899266435,
)
half_log2e = math.sqrt(0.5 * math.log2(math.e))


def params_of(megabytes):
    return pltpu.CompilerParams(vmem_limit_bytes=megabytes << 20)


def harmonics(ray_x, ray_y, ray_z):
    sq_x = ray_x * ray_x
    sq_y = ray_y * ray_y
    sq_z = ray_z * ray_z
    return jnp.stack(
        [
            band_zero * jnp.ones_like(ray_x),
            -band_one * ray_y,
            band_one * ray_z,
            -band_one * ray_x,
            band_two[0] * ray_x * ray_y,
            band_two[1] * ray_y * ray_z,
            band_two[2] * (2.0 * sq_z - sq_x - sq_y),
            band_two[3] * ray_x * ray_z,
            band_two[4] * (sq_x - sq_y),
            band_three[0] * ray_y * (3.0 * sq_x - sq_y),
            band_three[1] * ray_x * ray_y * ray_z,
            band_three[2] * ray_y * (4.0 * sq_z - sq_x - sq_y),
            band_three[3] * ray_z * (2.0 * sq_z - 3.0 * sq_x - 3.0 * sq_y),
            band_three[4] * ray_x * (4.0 * sq_z - sq_x - sq_y),
            band_three[5] * ray_z * (sq_x - sq_y),
            band_three[6] * ray_x * (sq_x - 3.0 * sq_y),
        ]
    )


def project(gauss_rows, camera_row):
    image_width = 1.0 * SIDE * IMG_TX
    image_height = 1.0 * SIDE * IMG_TY
    depth_z = gauss_rows[2]
    screen_u = (gauss_rows[0] - camera_row[0]) / depth_z
    screen_v = (gauss_rows[1] - camera_row[1]) / depth_z
    inv_one = depth_z * depth_z * jnp.exp(-2.0 * gauss_rows[3])
    inv_two = depth_z * depth_z * jnp.exp(-2.0 * gauss_rows[4])
    cosine = jnp.cos(gauss_rows[5])
    sine_angle = jnp.sin(gauss_rows[5])
    conic_a = cosine * cosine * inv_one + sine_angle * sine_angle * inv_two
    conic_b = cosine * sine_angle * (inv_one - inv_two)
    conic_c = sine_angle * sine_angle * inv_one + cosine * cosine * inv_two
    log_opacity = math.log(0.99) - jax.nn.softplus(-gauss_rows[6])
    ray_x = (screen_u - 0.5 * image_width) / image_width
    ray_y = (screen_v - 0.5 * image_height) / image_width
    factor = lax.rsqrt(ray_x * ray_x + ray_y * ray_y + 1.0)
    harmonic_basis = harmonics(ray_x * factor, ray_y * factor, factor)
    coeffs = gauss_rows[7:].reshape(3, NCOEF, gauss_rows.shape[1])
    colour = 0.5 + jnp.sum(coeffs * harmonic_basis[None], axis=1)
    geometry = jnp.stack([screen_u, screen_v, conic_a, conic_b, conic_c, log_opacity])
    return jnp.concatenate([geometry, colour], 0), (inv_one, inv_two)


def factor_rows(projected, inverses):
    conic_a, conic_b, conic_c = projected[2], projected[3], projected[4]
    inv_one, inv_two = inverses
    has_a = conic_a > 0.0
    safe_a = jnp.where(has_a, conic_a, 1.0)
    root = jnp.sqrt(safe_a)
    alpha = jnp.where(has_a, half_log2e * root, 0.0)
    beta = jnp.where(has_a, half_log2e * conic_b / root, 0.0)
    gamma = half_log2e * jnp.where(
        has_a, jnp.sqrt(inv_one * (inv_two / safe_a)), jnp.sqrt(conic_c)
    )
    log2_opacity = jnp.maximum(projected[5] * math.log2(math.e), -1.0e4)
    return jnp.concatenate(
        [projected[0:2], jnp.stack([alpha, beta, gamma, log2_opacity]), projected[6:9]], 0
    )


def split3(values):
    hi = values.astype(BF16).astype(F32)
    rest = values - hi
    mid = rest.astype(BF16).astype(F32)
    return hi, mid, rest - mid


def routing_kernel(ids_ref, tx_ref, ty_ref, upper_ref, slot_ref, want_ref, tile_ref):
    row_iota = lax.broadcasted_iota(I32, (OWN, LANES), 0)
    zero = jnp.zeros((OWN, LANES), F32)
    upper = upper_ref[...]

    def body(k, carry):
        out = []
        for s in range(STEPS):
            counts, acc = carry[s]
            ids = ids_ref[s, pl.ds(k, 1), :]
            owner = lax.shift_right_logical(ids, 11)
            member = row_iota == owner
            member_bf = jnp.where(member, 1.0, 0.0).astype(BF16)
            ahead = jnp.dot(member_bf, upper, preferred_element_type=F32)
            rank = jnp.sum(
                jnp.where(member, ahead[:, :LANES] + counts, 0.0), axis=0, keepdims=True
            ).astype(I32)
            counts = counts + ahead[:, LANES:]
            slot_ref[s, pl.ds(k, 1), :] = owner * LANES + rank
            here = row_iota == rank
            local = ids & 2047
            cells = [
                jnp.where(here, value, 0.0).astype(BF16)
                for value in (
                    (local & 127).astype(F32),
                    lax.shift_right_logical(local, 7).astype(F32),
                    tx_ref[s, 0:1, :],
                    ty_ref[s, 0:1, :],
                )
            ]
            acc = acc + lax.dot_general(
                member_bf,
                jnp.concatenate(cells, 0),
                (((1,), (1,)), ((), ())),
                preferred_element_type=F32,
            )
            out.append((counts, acc))
        return tuple(out)

    start = tuple((zero, jnp.zeros((OWN, 4 * LANES), F32)) for _ in range(STEPS))
    done = lax.fori_loop(0, SLABS, body, start, unroll=2)
    for s in range(STEPS):
        acc = done[s][1].astype(I32)
        want_ref[s] = acc[:, 0:128] + acc[:, 128:256] * 128
        tile_ref[s] = acc[:, 256:384] + acc[:, 384:512] * IMG_TX


def routing(ids, tile_x, tile_y):
    strict = np.triu(np.ones((128, 128), np.float32), 1)
    upper = jnp.asarray(np.concatenate([strict, np.ones((128, 128), np.float32)], 1), BF16)
    return pl.pallas_call(
        routing_kernel,
        out_shape=(
            jax.ShapeDtypeStruct((STEPS, SLABS, LANES), I32),
            jax.ShapeDtypeStruct((STEPS, OWN, LANES), I32),
            jax.ShapeDtypeStruct((STEPS, OWN, LANES), I32),
        ),
        compiler_params=params_of(32),
        name="routing",
    )(ids, tile_x, tile_y, upper)


def gather_kernel(table_ref, want_ref, tile_ref, out_ref, shift_ref, parts, got):
    for f in range(FIELDS):
        for p, part in enumerate(split3(table_ref[f])):
            parts[f * 16 : f * 16 + 16, p * 128 : p * 128 + 128] = part.astype(BF16)
    low_iota = lax.broadcasted_iota(I32, (128, 256), 0)
    high_iota = lax.broadcasted_iota(I32, (16, 256), 0)

    def body(c, _):
        want = jnp.concatenate(
            [want_ref[pl.ds(2 * c, 1), :], want_ref[pl.ds(2 * c + 1, 1), :]], 1
        )
        hot = jnp.where(low_iota == (want & 127), 1.0, 0.0).astype(BF16)
        hot = jnp.concatenate([hot, hot, hot], 0)
        here = high_iota == lax.shift_right_logical(want, 7)
        picked = jnp.dot(parts[...], hot, preferred_element_type=F32)
        for f in range(FIELDS):
            row = jnp.sum(
                jnp.where(here, picked[f * 16 : f * 16 + 16], 0.0), axis=0, keepdims=True
            )
            got[f, pl.ds(2 * c, 1), :] = row[:, :128]
            got[f, pl.ds(2 * c + 1, 1), :] = row[:, 128:]
        return 0

    lax.fori_loop(0, OWN // 2, body, 0, unroll=2)
    tile = tile_ref[...]
    centre_x = ((tile & (IMG_TX - 1)) * SIDE + SIDE // 2).astype(F32)
    centre_y = (lax.shift_right_logical(tile, 6) * SIDE + SIDE // 2).astype(F32)
    local_u = got[0] - centre_x
    local_v = got[1] - centre_y
    shift_ref[0] = local_u
    shift_ref[1] = local_v
    alpha, beta, gamma = got[2], got[3], got[4]
    out_ref[0] = alpha
    out_ref[1] = beta
    out_ref[2] = gamma
    out_ref[3] = -(alpha * local_u + beta * local_v)
    out_ref[4] = -gamma * local_v
    for f in range(5, FIELDS):
        out_ref[f] = got[f]


def owner_gather(table, want, tile):
    return pl.pallas_call(
        gather_kernel,
        out_shape=(
            jax.ShapeDtypeStruct((FIELDS, OWN, LANES), F32),
            jax.ShapeDtypeStruct((2, OWN, LANES), F32),
        ),
        scratch_shapes=[
            pltpu.VMEM((FIELDS * 16, 384), BF16),
            pltpu.VMEM((FIELDS, OWN, LANES), F32),
        ],
        compiler_params=params_of(32),
        name="owner_gather",
    )(table, want, tile)


def scatter_kernel(moment_ref, shift_ref, want_ref, out_ref, high, rest):
    local_u, local_v = shift_ref[0], shift_ref[1]
    m0, mx, my = moment_ref[0], moment_ref[1], moment_ref[2]
    sx = mx - local_u * m0
    sy = my - local_v * m0
    sums = [
        sx,
        sy,
        moment_ref[3] - local_u * (mx + sx),
        moment_ref[4] - local_u * my - local_v * sx,
        moment_ref[5] - local_v * (my + sy),
        m0,
        moment_ref[6],
        moment_ref[7],
        moment_ref[8],
    ]
    for f in range(FIELDS):
        top = sums[f].astype(BF16).astype(F32)
        high[f] = top
        rest[f] = sums[f] - top
    low_iota = lax.broadcasted_iota(I32, (128, 128), 0)
    high_iota = lax.broadcasted_iota(I32, (16, 128), 0)

    def body(c, acc):
        lefts, rights = [], []
        for half in range(2):
            d = 2 * c + half
            want = want_ref[pl.ds(d, 1), :]
            rights.append(jnp.where(low_iota == (want & 127), 1.0, 0.0).astype(BF16))
            here = high_iota == lax.shift_right_logical(want, 7)
            rows = [
                jnp.where(here, ref[f, pl.ds(d, 1), :], 0.0).astype(BF16)
                for ref in (high, rest)
                for f in range(FIELDS)
            ]
            lefts.append(jnp.concatenate(rows, 0))
        return acc + lax.dot_general(
            jnp.concatenate(lefts, 1),
            jnp.concatenate(rights, 1),
            (((1,), (1,)), ((), ())),
            preferred_element_type=F32,
        )

    acc = lax.fori_loop(
        0, OWN // 2, body, jnp.zeros((2 * FIELDS * 16, 128), F32), unroll=2
    )
    out_ref[...] = acc[: FIELDS * 16] + acc[FIELDS * 16 :]


def owner_scatter(moments, shifts, want):
    return pl.pallas_call(
        scatter_kernel,
        out_shape=jax.ShapeDtypeStruct((FIELDS * 16, 128), F32),
        scratch_shapes=[
            pltpu.VMEM((FIELDS, OWN, LANES), F32),
            pltpu.VMEM((FIELDS, OWN, LANES), F32),
        ],
        compiler_params=params_of(32),
        name="owner_scatter",
    )(moments, shifts, want)


def render_constants():
    axis = np.arange(SIDE, dtype=np.float32) - 7.5
    x = np.tile(axis, SIDE)
    y = np.repeat(axis, SIDE)
    one = np.ones_like(x)
    zero = np.zeros_like(x)
    block = np.zeros((8, 512), np.float32)
    block[0] = np.concatenate([x, zero])
    block[1] = np.concatenate([y, zero])
    block[2] = np.concatenate([zero, y])
    block[3] = np.concatenate([one, zero])
    block[4] = np.concatenate([zero, one])
    lines = np.concatenate([block, block, block, np.zeros_like(block)], 0)
    mono = np.zeros((PIX, 128), np.float32)
    for k, column in enumerate((one, x, y, x * x, x * y, y * y)):
        mono[:, k] = column
    return jnp.asarray(lines, BF16), jnp.asarray(mono, BF16)


COL_OPACITY = 29


def render_kernel(
    slot_ref, fields_ref, target_ref, lines_ref, mono_ref,
    picture_ref, moment_ref, loss_ref,
    table, rows, line_a, line_b, alphas, weights, out_a, out_b, resid, back,
):
    def build(o, _):
        first = fields_ref[0:8, pl.ds(o, 1), :].reshape(8, LANES)
        last = jnp.broadcast_to(fields_ref[8, pl.ds(o, 1), :], (8, LANES))
        stack = jnp.concatenate([*split3(first), first, last], 0)
        table[pl.ds(pl.multiple_of(o * 128, 128), 128), 0:40] = stack.T
        return 0

    lax.fori_loop(0, OWN, build, 0, unroll=4)

    def zero_out(o, _):
        back[pl.ds(pl.multiple_of(o * 128, 128), 128), :] = jnp.zeros((128, LANES), F32)
        return 0

    lax.fori_loop(0, OWN, zero_out, 0)

    def fetch(slab, i):
        source = jnp.minimum(slab, SLABS - 1)
        for t in range(TILES_DEV):
            q = i * TILES_DEV + t
            rows[pl.ds(pl.multiple_of(slab * 128, 128) + q, 1), :] = table[
                pl.ds(slot_ref[source * 128 + q], 1), :
            ]

    def lines_of(slab, line):
        left = rows[pl.ds(pl.multiple_of(slab * 128, 128), 128), 0:32].astype(BF16)
        line[...] = jnp.dot(left, lines_ref[...], preferred_element_type=F32)

    def forward(slab, line, state):
        through, red, green, blue = state
        for i in range(8):
            at = pl.ds(pl.multiple_of(slab * 128, 128) + i * 16, 16)
            first = line[i * 16 : i * 16 + 16, 0:256]
            second = line[i * 16 : i * 16 + 16, 256:512]
            cols = rows[at, COL_OPACITY : COL_OPACITY + 4]
            alpha = jnp.exp2(cols[:, 0:1] - first * first - second * second)
            weight = through * alpha
            through = through - weight
            red = red + weight * cols[:, 1:2]
            green = green + weight * cols[:, 2:3]
            blue = blue + weight * cols[:, 3:4]
            alphas[at, :] = alpha
            weights[at, :] = weight
            fetch(slab + 2, i)
        return through, red, green, blue

    for slab in range(2):
        for i in range(8):
            fetch(slab, i)
    lines_of(0, line_a)

    def forward_pair(pair, state):
        lines_of(2 * pair + 1, line_b)
        state = forward(2 * pair, line_a, state)
        lines_of(2 * pair + 2, line_a)
        return forward(2 * pair + 1, line_b, state)

    blank = jnp.zeros((TILES_DEV, PIX), F32)
    _, red, green, blue = lax.fori_loop(
        0, SLABS // 2, forward_pair, (jnp.ones((TILES_DEV, PIX), F32), blank, blank, blank)
    )
    residuals = []
    total = jnp.zeros((), F32)
    for ch, colour in enumerate((red, green, blue)):
        picture_ref[ch] = colour
        residual = colour - target_ref[ch]
        residuals.append(residual)
        total = total + jnp.sum(residual * residual)
    loss_ref[...] = jnp.full((1, LANES), 0.5 * total, F32)
    res_red, res_green, res_blue = residuals

    padded = jnp.concatenate([jnp.zeros((16, PIX), F32), *residuals, jnp.zeros((64, PIX), F32)], 0)
    turned = padded.T
    top = turned.astype(BF16)
    resid[:, 0:128] = top
    resid[:, 128:256] = (turned - top.astype(F32)).astype(BF16)

    lane = lax.broadcasted_iota(I32, (128, LANES), 1)
    row = lax.broadcasted_iota(I32, (128, LANES), 0)
    own_tile = (lane & 15) == (row & 15)

    def scatter(slab, i, source):
        for t in range(TILES_DEV):
            q = i * TILES_DEV + t
            back[pl.ds(slot_ref[slab * 128 + q], 1), :] = source[q : q + 1, :]

    def backward(slab, behind, target, previous, source):
        pieces = [None] * 8
        for i in range(7, -1, -1):
            at = pl.ds(pl.multiple_of(slab * 128, 128) + i * 16, 16)
            cols = rows[at, COL_OPACITY : COL_OPACITY + 4]
            alpha = alphas[at, :]
            gain = (
                res_red * cols[:, 1:2] + res_green * cols[:, 2:3] + res_blue * cols[:, 3:4]
            ) - behind
            pieces[i] = weights[at, :] * gain
            behind = behind + alpha * gain
            if source is not None:
                scatter(previous, i, source)
        slope = jnp.concatenate(pieces, 0)
        slope_top = slope.astype(BF16)
        slope_rest = (slope - slope_top.astype(F32)).astype(BF16)
        weight = weights[pl.ds(pl.multiple_of(slab * 128, 128), 128), :]
        weight_top = weight.astype(BF16)
        weight_rest = (weight - weight_top.astype(F32)).astype(BF16)
        moment = jnp.dot(slope_top, mono_ref[...], preferred_element_type=F32)
        moment = moment + jnp.dot(slope_rest, mono_ref[...], preferred_element_type=F32)
        both = jnp.dot(weight_top, resid[...], preferred_element_type=F32)
        shade = both[:, :128] + both[:, 128:]
        shade = shade + jnp.dot(weight_rest, resid[:, 0:128], preferred_element_type=F32)
        target[...] = moment + jnp.where(own_tile, shade, 0.0)
        return behind

    behind = backward(SLABS - 1, blank, out_a, None, None)

    def backward_pair(pair, behind):
        slab = SLABS - 2 - 2 * pair
        behind = backward(slab, behind, out_b, slab + 1, out_a)
        return backward(slab - 1, behind, out_a, slab, out_b)

    behind = lax.fori_loop(0, SLABS // 2 - 1, backward_pair, behind)
    backward(0, behind, out_b, 1, out_a)
    for i in range(8):
        scatter(0, i, out_b)

    def finish(o, _):
        turned = back[pl.ds(pl.multiple_of(o * 128, 128), 128), 0:64].T
        for k in range(6):
            moment_ref[k, pl.ds(o, 1), :] = turned[k : k + 1]
        for ch in range(3):
            part = turned[16 + 16 * ch : 32 + 16 * ch]
            moment_ref[6 + ch, pl.ds(o, 1), :] = jnp.sum(part, axis=0, keepdims=True)
        return 0

    lax.fori_loop(0, OWN, finish, 0, unroll=4)


def render(slots, fields, target):
    lines, mono = render_constants()
    vmem = pl.BlockSpec(memory_space=pltpu.VMEM)
    entries = SLABS * 128
    return pl.pallas_call(
        render_kernel,
        out_shape=(
            jax.ShapeDtypeStruct((3, TILES_DEV, PIX), F32),
            jax.ShapeDtypeStruct((FIELDS, OWN, LANES), F32),
            jax.ShapeDtypeStruct((1, LANES), F32),
        ),
        in_specs=[pl.BlockSpec(memory_space=pltpu.SMEM)] + [vmem] * 4,
        out_specs=(vmem, vmem, vmem),
        scratch_shapes=[
            pltpu.VMEM((OWN * LANES, LANES), F32),
            pltpu.VMEM((entries + 256, LANES), F32),
            pltpu.VMEM((128, 512), F32),
            pltpu.VMEM((128, 512), F32),
            pltpu.VMEM((entries, PIX), F32),
            pltpu.VMEM((entries, PIX), F32),
            pltpu.VMEM((128, LANES), F32),
            pltpu.VMEM((128, LANES), F32),
            pltpu.VMEM((PIX, 256), BF16),
            pltpu.VMEM((OWN * LANES, LANES), F32),
        ],
        compiler_params=params_of(56),
        name="render",
    )(slots, fields, target, lines, mono)


def exchange(blocks):
    return lax.all_to_all(blocks, ("gx", "gy"), split_axis=1, concat_axis=1, tiled=True)


def adam_update(params, moment_one, second, gradient, step_index):
    step_count = adam_start + step_index + 1
    moment_one = beta_one * moment_one + (1.0 - beta_one) * gradient
    second = beta_two * second + (1.0 - beta_two) * gradient * gradient
    scaled_first = moment_one / (1.0 - beta_one**step_count)
    scaled_second = second / (1.0 - beta_two**step_count)
    params = params - learn_rate * scaled_first / (jnp.sqrt(scaled_second) + adam_eps)
    return (params, moment_one, second)


def per_device(gauss_params, first_moment, second_moment, splat_lists, tile_ids, targets, camera):
    local_count = gauss_params.shape[1]
    params, moment_one, moment_two = (gauss_params, first_moment, second_moment)
    ids = jnp.swapaxes(splat_lists, 1, 2).reshape(STEPS, SLABS, LANES)
    lane_tiles = jnp.tile(tile_ids, (1, LANES // TILES_DEV))
    tile_x = (lane_tiles % IMG_TX).astype(F32)[:, None, :]
    tile_y = (lane_tiles // IMG_TX).astype(F32)[:, None, :]
    slots, want, tiles = routing(ids, tile_x, tile_y)
    slots = slots.reshape(STEPS, SLABS * LANES)
    asked = exchange(jnp.concatenate([want, tiles], 0))
    pictures = []
    losses = []
    for step_index in range(STEPS):
        wanted, wanted_tile = asked[step_index], asked[STEPS + step_index]
        projected, pullback, inverses = jax.vjp(
            lambda values: project(values, camera[step_index]), params, has_aux=True
        )
        table = factor_rows(projected, inverses).reshape(FIELDS, 16, 128)
        fields, shifts = owner_gather(table, wanted, wanted_tile)
        fields = exchange(fields)
        target = jnp.swapaxes(targets[step_index], 0, 1)
        picture, moments, loss = render(slots[step_index], fields, target)
        extra = jnp.broadcast_to(loss[None], (1, OWN, LANES))
        arrived = exchange(jnp.concatenate([moments, extra], 0))
        losses.append(jnp.sum(arrived[FIELDS, :, 0]))
        sums = owner_scatter(arrived, shifts, wanted).reshape(FIELDS, local_count)
        conic_a, conic_b, conic_c = projected[2], projected[3], projected[4]
        cotangent = jnp.concatenate(
            [
                jnp.stack(
                    [
                        conic_a * sums[0] + conic_b * sums[1],
                        conic_b * sums[0] + conic_c * sums[1],
                        -0.5 * sums[2],
                        -sums[3],
                        -0.5 * sums[4],
                    ]
                ),
                sums[5:9],
            ],
            0,
        )
        gradient = pullback(cotangent)[0]
        params, moment_one, moment_two = adam_update(
            params, moment_one, moment_two, gradient, step_index
        )
        pictures.append(jnp.swapaxes(picture, 0, 1))
    loss_values = jnp.stack(losses) / (3.0 * PIX * TILES_DEV * OWN)
    return (params, moment_one, moment_two, jnp.stack(pictures), loss_values)


def solution(mesh):
    both = ("gx", "gy")
    in_specs = (
        P(None, both),
        P(None, both),
        P(None, both),
        P(None, both, None),
        P(None, both),
        P(None, both, None, None),
        P(),
    )
    out_specs = (
        P(None, both),
        P(None, both),
        P(None, both),
        P(None, both, None, None),
        P(),
    )
    return jax.shard_map(
        per_device, mesh=mesh, in_specs=in_specs, out_specs=out_specs, check_vma=False
    )
```

```python
import functools
import math

import jax
import jax.numpy as jnp
import numpy as np
from jax import lax
from jax.experimental import pallas as pl
from jax.experimental.pallas import tpu as pltpu
from jax.sharding import PartitionSpec as P

SIDE = 16
PIX = 256
NCOEF = 16
STEPS = 2
IMG_TX = 64
IMG_TY = 32
OWN = 128
LANES = 128
TILES_DEV = 16
LIST = 512
SLABS = LIST * TILES_DEV // 128
FIELDS = 9
F32 = jnp.float32
BF16 = jnp.bfloat16
I32 = jnp.int32

beta_one = 0.9
beta_two = 0.999
adam_eps = 1e-08
learn_rate = 0.01
adam_start = 1000
band_zero = 0.28209479177387814
band_one = 0.4886025119029199
band_two = (
    1.0925484305920792,
    -1.0925484305920792,
    0.31539156525252005,
    -1.0925484305920792,
    0.5462742152960396,
)
band_three = (
    -0.5900435899266435,
    2.890611442640554,
    -0.4570457994644658,
    0.3731763325901154,
    -0.4570457994644658,
    1.445305721320277,
    -0.5900435899266435,
)
half_log2e = math.sqrt(0.5 * math.log2(math.e))


def params_of(megabytes):
    return pltpu.CompilerParams(vmem_limit_bytes=megabytes << 20)


def harmonics(ray_x, ray_y, ray_z):
    sq_x = ray_x * ray_x
    sq_y = ray_y * ray_y
    sq_z = ray_z * ray_z
    return jnp.stack(
        [
            band_zero * jnp.ones_like(ray_x),
            -band_one * ray_y,
            band_one * ray_z,
            -band_one * ray_x,
            band_two[0] * ray_x * ray_y,
            band_two[1] * ray_y * ray_z,
            band_two[2] * (2.0 * sq_z - sq_x - sq_y),
            band_two[3] * ray_x * ray_z,
            band_two[4] * (sq_x - sq_y),
            band_three[0] * ray_y * (3.0 * sq_x - sq_y),
            band_three[1] * ray_x * ray_y * ray_z,
            band_three[2] * ray_y * (4.0 * sq_z - sq_x - sq_y),
            band_three[3] * ray_z * (2.0 * sq_z - 3.0 * sq_x - 3.0 * sq_y),
            band_three[4] * ray_x * (4.0 * sq_z - sq_x - sq_y),
            band_three[5] * ray_z * (sq_x - sq_y),
            band_three[6] * ray_x * (sq_x - 3.0 * sq_y),
        ]
    )


def project(gauss_rows, camera_row):
    image_width = 1.0 * SIDE * IMG_TX
    image_height = 1.0 * SIDE * IMG_TY
    depth_z = gauss_rows[2]
    screen_u = (gauss_rows[0] - camera_row[0]) / depth_z
    screen_v = (gauss_rows[1] - camera_row[1]) / depth_z
    inv_one = depth_z * depth_z * jnp.exp(-2.0 * gauss_rows[3])
    inv_two = depth_z * depth_z * jnp.exp(-2.0 * gauss_rows[4])
    cosine = jnp.cos(gauss_rows[5])
    sine_angle = jnp.sin(gauss_rows[5])
    conic_a = cosine * cosine * inv_one + sine_angle * sine_angle * inv_two
    conic_b = cosine * sine_angle * (inv_one - inv_two)
    conic_c = sine_angle * sine_angle * inv_one + cosine * cosine * inv_two
    log_opacity = math.log(0.99) - jax.nn.softplus(-gauss_rows[6])
    ray_x = (screen_u - 0.5 * image_width) / image_width
    ray_y = (screen_v - 0.5 * image_height) / image_width
    factor = lax.rsqrt(ray_x * ray_x + ray_y * ray_y + 1.0)
    harmonic_basis = harmonics(ray_x * factor, ray_y * factor, factor)
    coeffs = gauss_rows[7:].reshape(3, NCOEF, gauss_rows.shape[1])
    colour = 0.5 + jnp.sum(coeffs * harmonic_basis[None], axis=1)
    geometry = jnp.stack([screen_u, screen_v, conic_a, conic_b, conic_c, log_opacity])
    return jnp.concatenate([geometry, colour], 0), (inv_one, inv_two)


def factor_rows(projected, inverses):
    conic_a, conic_b, conic_c = projected[2], projected[3], projected[4]
    inv_one, inv_two = inverses
    has_a = conic_a > 0.0
    safe_a = jnp.where(has_a, conic_a, 1.0)
    root = jnp.sqrt(safe_a)
    alpha = jnp.where(has_a, half_log2e * root, 0.0)
    beta = jnp.where(has_a, half_log2e * conic_b / root, 0.0)
    gamma = half_log2e * jnp.where(
        has_a, jnp.sqrt(inv_one * (inv_two / safe_a)), jnp.sqrt(conic_c)
    )
    log2_opacity = jnp.maximum(projected[5] * math.log2(math.e), -1.0e4)
    return jnp.concatenate(
        [projected[0:2], jnp.stack([alpha, beta, gamma, log2_opacity]), projected[6:9]], 0
    )


def split3(values):
    hi = values.astype(BF16).astype(F32)
    rest = values - hi
    mid = rest.astype(BF16).astype(F32)
    return hi, mid, rest - mid


def my_index():
    return lax.axis_index("gx") * lax.axis_size("gy") + lax.axis_index("gy")


def mesh_place(device):
    inner = lax.axis_size("gy")
    return (device // inner, lax.rem(device, inner))


def greet():
    barrier = pltpu.get_barrier_semaphore()
    me = my_index()

    def one(k, _):
        pl.semaphore_signal(
            barrier,
            inc=1,
            device_id=mesh_place(lax.rem(me + k, OWN)),
            device_id_type=pl.DeviceIdType.MESH,
        )
        return 0

    lax.fori_loop(1, OWN, one, 0, unroll=2)


def all_entered():
    pl.semaphore_wait(pltpu.get_barrier_semaphore(), OWN - 1)


def send(source, target, peer, send_sem, recv_sem):
    me = my_index()
    pltpu.make_async_remote_copy(
        src_ref=source.at[:, peer, :],
        dst_ref=target.at[:, me, :],
        send_sem=send_sem,
        recv_sem=recv_sem,
        device_id=mesh_place(peer),
        device_id_type=pl.DeviceIdType.MESH,
    ).start()


def all_but_one(source, target, send_sem, recv_sem):
    blocks = pl.ds(0, OWN - 1)
    return pltpu.make_async_remote_copy(
        src_ref=source.at[:, blocks, :],
        dst_ref=target.at[:, blocks, :],
        send_sem=send_sem,
        recv_sem=recv_sem,
        device_id=mesh_place(my_index()),
        device_id_type=pl.DeviceIdType.MESH,
    )


def keep_own(source, target):
    me = my_index()
    for k in range(source.shape[0]):
        target[k, pl.ds(me, 1), :] = source[k, pl.ds(me, 1), :]


def remote_params(collective_id, megabytes=32):
    return pltpu.CompilerParams(
        collective_id=collective_id, has_side_effects=True, vmem_limit_bytes=megabytes << 20
    )


GROUP = 4


def routing_kernel(ids_ref, tile_ref, upper_ref, slot_ref, asked_ref, request, send_sem, recv_sem):
    greet()
    row_iota = lax.broadcasted_iota(I32, (OWN, LANES), 0)
    own_tile = (lax.broadcasted_iota(I32, (1, LANES), 1) & (TILES_DEV - 1)).astype(F32)
    zero = jnp.zeros((OWN, LANES), F32)
    upper = upper_ref[...]

    def body(k, carry):
        out = []
        for s in range(STEPS):
            counts, acc = carry[s]
            members, cells = [], []
            for c in range(GROUP):
                ids = ids_ref[s, pl.ds(k * GROUP + c, 1), :]
                owner = lax.shift_right_logical(ids, 11)
                member = row_iota == owner
                member_bf = jnp.where(member, 1.0, 0.0).astype(BF16)
                ahead = jnp.dot(member_bf, upper, preferred_element_type=F32)
                rank = jnp.sum(
                    jnp.where(member, ahead[:, :LANES] + counts, 0.0), axis=0, keepdims=True
                ).astype(I32)
                counts = counts + ahead[:, LANES:]
                slot_ref[s, pl.ds(k * GROUP + c, 1), :] = owner * LANES + rank
                here = row_iota == rank
                low = (ids & 127).astype(F32)
                high = (lax.shift_right_logical(ids, 7) & 15).astype(F32) * 16.0 + own_tile
                members.append(member_bf)
                cells.append(
                    jnp.concatenate(
                        [
                            jnp.where(here, low, 0.0).astype(BF16),
                            jnp.where(here, high, 0.0).astype(BF16),
                        ],
                        0,
                    )
                )
            acc = acc + lax.dot_general(
                jnp.concatenate(members, 1),
                jnp.concatenate(cells, 1),
                (((1,), (1,)), ((), ())),
                preferred_element_type=F32,
            )
            out.append((counts, acc))
        return tuple(out)

    start = tuple((zero, jnp.zeros((OWN, 2 * LANES), F32)) for _ in range(STEPS))
    done = lax.fori_loop(0, SLABS // GROUP, body, start)
    for s in range(STEPS):
        acc = done[s][1].astype(I32)
        high = acc[:, LANES:]
        request[s] = acc[:, :LANES] + lax.shift_right_logical(high, 4) * 128
        request[STEPS + s] = jnp.take_along_axis(
            jnp.broadcast_to(tile_ref[s], (OWN, LANES)),
            high & 15,
            axis=1,
            mode="promise_in_bounds",
        )
    all_entered()
    me = my_index()

    def push(k, _):
        send(request, asked_ref, lax.rem(me + k, OWN), send_sem, recv_sem)
        return 0

    lax.fori_loop(1, OWN, push, 0, unroll=2)
    keep_own(request, asked_ref)
    rest = all_but_one(request, asked_ref, send_sem, recv_sem)
    rest.wait_send()
    rest.wait_recv()


def routing(ids, lane_tiles):
    strict = np.triu(np.ones((128, 128), np.float32), 1)
    upper = jnp.asarray(np.concatenate([strict, np.ones((128, 128), np.float32)], 1), BF16)
    vmem = pl.BlockSpec(memory_space=pltpu.VMEM)
    return pl.pallas_call(
        routing_kernel,
        out_shape=(
            jax.ShapeDtypeStruct((STEPS, SLABS, LANES), I32),
            jax.ShapeDtypeStruct((2 * STEPS, OWN, LANES), I32),
        ),
        in_specs=[vmem] * 3,
        out_specs=(vmem, vmem),
        scratch_shapes=[
            pltpu.VMEM((2 * STEPS, OWN, LANES), I32),
            pltpu.SemaphoreType.DMA,
            pltpu.SemaphoreType.DMA,
        ],
        compiler_params=remote_params(0),
        name="routing",
    )(ids, lane_tiles, upper)


BLOCKS = 8


def gather_kernel(
    step, table_ref, asked_ref, out_ref, shift_ref, parts, got, answer, send_sem, recv_sem
):
    greet()
    for f in range(FIELDS):
        for p, part in enumerate(split3(table_ref[f])):
            parts[f * 16 : f * 16 + 16, p * 128 : p * 128 + 128] = part.astype(BF16)
    low_iota = lax.broadcasted_iota(I32, (128, 256), 0)
    high_iota = lax.broadcasted_iota(I32, (16, 256), 0)
    me = my_index()
    groups = OWN // BLOCKS

    def group_of(k):
        return lax.rem(me // BLOCKS + k, groups)

    def compute(group):
        first = pl.multiple_of(group * BLOCKS, BLOCKS)
        for pair in range(BLOCKS // 2):
            d = first + 2 * pair
            want = jnp.concatenate(
                [asked_ref[step, pl.ds(d, 1), :], asked_ref[step, pl.ds(d + 1, 1), :]], 1
            )
            hot = jnp.where(low_iota == (want & 127), 1.0, 0.0).astype(BF16)
            hot = jnp.concatenate([hot, hot, hot], 0)
            here = high_iota == lax.shift_right_logical(want, 7)
            picked = jnp.dot(parts[...], hot, preferred_element_type=F32)
            for f in range(FIELDS):
                row = jnp.sum(
                    jnp.where(here, picked[f * 16 : f * 16 + 16], 0.0), axis=0, keepdims=True
                )
                got[f, 2 * pair : 2 * pair + 1, :] = row[:, :128]
                got[f, 2 * pair + 1 : 2 * pair + 2, :] = row[:, 128:]
        at = pl.ds(first, BLOCKS)
        tile = asked_ref[STEPS + step, at, :]
        centre_x = ((tile & (IMG_TX - 1)) * SIDE + SIDE // 2).astype(F32)
        centre_y = (lax.shift_right_logical(tile, 6) * SIDE + SIDE // 2).astype(F32)
        local_u = got[0] - centre_x
        local_v = got[1] - centre_y
        shift_ref[0, at, :] = local_u
        shift_ref[1, at, :] = local_v
        alpha, beta, gamma = got[2], got[3], got[4]
        answer[0, at, :] = alpha
        answer[1, at, :] = beta
        answer[2, at, :] = gamma
        answer[3, at, :] = -(alpha * local_u + beta * local_v)
        answer[4, at, :] = -gamma * local_v
        for f in range(5, FIELDS):
            answer[f, at, :] = got[f]

    def push(group):
        def one(k, _):
            peer = group * BLOCKS + lax.rem(me + k, BLOCKS)

            @pl.when(peer != me)
            def _():
                send(answer, out_ref, peer, send_sem, recv_sem)

            return 0

        lax.fori_loop(0, BLOCKS, one, 0)

    def early(k, _):
        compute(group_of(k))
        return 0

    lax.fori_loop(0, groups // 2, early, 0)
    all_entered()

    def late(k, _):
        push(group_of(k))
        compute(group_of(k + groups // 2))
        return 0

    lax.fori_loop(0, groups // 2, late, 0)

    def last(k, _):
        push(group_of(k + groups // 2))
        return 0

    lax.fori_loop(0, groups // 2, last, 0)
    keep_own(answer, out_ref)
    rest = all_but_one(answer, out_ref, send_sem, recv_sem)
    rest.wait_send()
    rest.wait_recv()


def owner_gather(step, table, asked):
    vmem = pl.BlockSpec(memory_space=pltpu.VMEM)
    return pl.pallas_call(
        functools.partial(gather_kernel, step),
        out_shape=(
            jax.ShapeDtypeStruct((FIELDS, OWN, LANES), F32),
            jax.ShapeDtypeStruct((2, OWN, LANES), F32),
        ),
        in_specs=[vmem] * 2,
        out_specs=(vmem, vmem),
        scratch_shapes=[
            pltpu.VMEM((FIELDS * 16, 384), BF16),
            pltpu.VMEM((FIELDS, BLOCKS, LANES), F32),
            pltpu.VMEM((FIELDS, OWN, LANES), F32),
            pltpu.SemaphoreType.DMA,
            pltpu.SemaphoreType.DMA,
        ],
        compiler_params=remote_params(1 + step),
        name="owner_gather",
    )(table, asked)


def scatter_kernel(
    step, moment_ref, shift_ref, asked_ref, out_ref, loss_ref,
    arrived, high, rest, own_sem, send_sem, recv_sems,
):
    greet()
    me = my_index()
    groups = OWN // BLOCKS
    mine = me // BLOCKS
    all_entered()

    def push(k, _):
        send(moment_ref, arrived, lax.rem(me + k, OWN), send_sem, recv_sems.at[mine])
        return 0

    lax.fori_loop(1, OWN, push, 0, unroll=2)
    own = pltpu.make_async_copy(moment_ref.at[:, me, :], arrived.at[:, me, :], own_sem)
    own.start()
    own.wait()
    low_iota = lax.broadcasted_iota(I32, (128, 128), 0)
    high_iota = lax.broadcasted_iota(I32, (16, 128), 0)

    def landed(group, count):
        blocks = pl.ds(group * BLOCKS, count)
        pltpu.make_async_remote_copy(
            src_ref=moment_ref.at[:, blocks, :],
            dst_ref=arrived.at[:, blocks, :],
            send_sem=send_sem,
            recv_sem=recv_sems.at[group],
            device_id=mesh_place(me),
            device_id_type=pl.DeviceIdType.MESH,
        ).wait_recv()

    def body(k, carry):
        acc, loss = carry
        group = lax.rem(mine + groups - k, groups)

        @pl.when(k == 0)
        def _():
            landed(group, BLOCKS - 1)

        @pl.when(k != 0)
        def _():
            landed(group, BLOCKS)

        first = pl.multiple_of(group * BLOCKS, BLOCKS)
        at = pl.ds(first, BLOCKS)
        local_u, local_v = shift_ref[0, at, :], shift_ref[1, at, :]
        m0, mx, my = arrived[0, at, :], arrived[1, at, :], arrived[2, at, :]
        sx = mx - local_u * m0
        sy = my - local_v * m0
        sums = [
            sx,
            sy,
            arrived[3, at, :] - local_u * (mx + sx),
            arrived[4, at, :] - local_u * my - local_v * sx,
            arrived[5, at, :] - local_v * (my + sy),
            m0,
            arrived[6, at, :],
            arrived[7, at, :],
            arrived[8, at, :],
        ]
        for f in range(FIELDS):
            top = sums[f].astype(BF16).astype(F32)
            high[f] = top
            rest[f] = sums[f] - top
        for pair in range(BLOCKS // 2):
            lefts, rights = [], []
            for half in range(2):
                d = 2 * pair + half
                want = asked_ref[step, pl.ds(first + d, 1), :]
                rights.append(jnp.where(low_iota == (want & 127), 1.0, 0.0).astype(BF16))
                here = high_iota == lax.shift_right_logical(want, 7)
                rows = [
                    jnp.where(here, ref[f, d : d + 1, :], 0.0).astype(BF16)
                    for ref in (high, rest)
                    for f in range(FIELDS)
                ]
                lefts.append(jnp.concatenate(rows, 0))
            acc = acc + lax.dot_general(
                jnp.concatenate(lefts, 1),
                jnp.concatenate(rights, 1),
                (((1,), (1,)), ((), ())),
                preferred_element_type=F32,
            )
        return acc, loss + arrived[FIELDS, at, :]

    acc, loss = lax.fori_loop(
        0,
        groups,
        body,
        (jnp.zeros((2 * FIELDS * 16, 128), F32), jnp.zeros((BLOCKS, LANES), F32)),
    )
    out_ref[...] = acc[: FIELDS * 16] + acc[FIELDS * 16 :]
    loss_ref[...] = jnp.sum(loss, axis=0, keepdims=True)
    all_but_one(moment_ref, arrived, send_sem, own_sem).wait_send()


def owner_scatter(step, moments, shifts, asked):
    vmem = pl.BlockSpec(memory_space=pltpu.VMEM)
    return pl.pallas_call(
        functools.partial(scatter_kernel, step),
        out_shape=(
            jax.ShapeDtypeStruct((FIELDS * 16, 128), F32),
            jax.ShapeDtypeStruct((1, LANES), F32),
        ),
        in_specs=[vmem] * 3,
        out_specs=(vmem, vmem),
        scratch_shapes=[
            pltpu.VMEM((FIELDS + 1, OWN, LANES), F32),
            pltpu.VMEM((FIELDS, BLOCKS, LANES), F32),
            pltpu.VMEM((FIELDS, BLOCKS, LANES), F32),
            pltpu.SemaphoreType.DMA,
            pltpu.SemaphoreType.DMA,
            pltpu.SemaphoreType.DMA((OWN // BLOCKS,)),
        ],
        compiler_params=remote_params(1 + STEPS + step),
        name="owner_scatter",
    )(moments, shifts, asked)


def render_constants():
    axis = np.arange(SIDE, dtype=np.float32) - 7.5
    x = np.tile(axis, SIDE)
    y = np.repeat(axis, SIDE)
    one = np.ones_like(x)
    zero = np.zeros_like(x)
    block = np.zeros((8, 512), np.float32)
    block[0] = np.concatenate([x, zero])
    block[1] = np.concatenate([y, zero])
    block[2] = np.concatenate([zero, y])
    block[3] = np.concatenate([one, zero])
    block[4] = np.concatenate([zero, one])
    lines = np.concatenate([block, block, block, np.zeros_like(block)], 0)
    mono = np.zeros((PIX, 128), np.float32)
    for k, column in enumerate((one, x, y, x * x, x * y, y * y)):
        mono[:, k] = column
    return jnp.asarray(lines, BF16), jnp.asarray(mono, BF16)


COL_OPACITY = 29


def render_kernel(
    slot_ref, fields_ref, target_ref, lines_ref, mono_ref,
    picture_ref, moment_ref,
    table, rows, alphas, weights, out_a, out_b, resid, back,
):
    def build(o, _):
        first = fields_ref[0:8, pl.ds(o, 1), :].reshape(8, LANES)
        last = jnp.broadcast_to(fields_ref[8, pl.ds(o, 1), :], (8, LANES))
        stack = jnp.concatenate([*split3(first), first, last], 0)
        table[pl.ds(pl.multiple_of(o * 128, 128), 128), 0:40] = stack.T
        return 0

    lax.fori_loop(0, OWN, build, 0, unroll=4)

    def zero_out(o, _):
        back[pl.ds(pl.multiple_of(o * 128, 128), 128), :] = jnp.zeros((128, LANES), F32)
        return 0

    lax.fori_loop(0, OWN, zero_out, 0)

    sublane = lax.broadcasted_iota(I32, (8, LANES), 0)

    def fetch(slab, i):
        source = jnp.minimum(slab, SLABS - 1) * 128 + i * TILES_DEV
        for half in range(0, TILES_DEV, 8):
            got = None
            for t in range(8):
                row = table[pl.ds(slot_ref[source + half + t], 1), :]
                row = jnp.broadcast_to(row, (8, LANES))
                got = row if t == 0 else jnp.where(sublane == t, row, got)
            at = pl.multiple_of(slab * 128, 128) + i * TILES_DEV + half
            rows[pl.ds(at, 8), :] = got

    def forward(slab, state):
        through, red, green, blue = state
        for i in range(8):
            at = pl.ds(pl.multiple_of(slab * 128, 128) + i * 16, 16)
            both = jnp.dot(
                rows[at, 0:32].astype(BF16), lines_ref[...], preferred_element_type=F32
            )
            first = both[:, 0:256]
            second = both[:, 256:512]
            cols = rows[at, COL_OPACITY : COL_OPACITY + 4]
            alpha = jnp.exp2(cols[:, 0:1] - first * first - second * second)
            weight = through * alpha
            through = through - weight
            red = red + weight * cols[:, 1:2]
            green = green + weight * cols[:, 2:3]
            blue = blue + weight * cols[:, 3:4]
            alphas[at, :] = alpha
            weights[at, :] = weight
            fetch(slab + 1, i)
        return through, red, green, blue

    for i in range(8):
        fetch(0, i)
    blank = jnp.zeros((TILES_DEV, PIX), F32)
    _, red, green, blue = lax.fori_loop(
        0,
        SLABS,
        forward,
        (jnp.ones((TILES_DEV, PIX), F32), blank, blank, blank),
        unroll=4,
    )
    residuals = []
    total = jnp.zeros((), F32)
    for ch, colour in enumerate((red, green, blue)):
        picture_ref[ch] = colour
        residual = colour - target_ref[ch]
        residuals.append(residual)
        total = total + jnp.sum(residual * residual)
    moment_ref[FIELDS] = jnp.full((OWN, LANES), 0.5 * total, F32)
    res_red, res_green, res_blue = residuals

    padded = jnp.concatenate([jnp.zeros((16, PIX), F32), *residuals, jnp.zeros((64, PIX), F32)], 0)
    turned = padded.T
    top = turned.astype(BF16)
    resid[:, 0:128] = top
    resid[:, 128:256] = (turned - top.astype(F32)).astype(BF16)

    lane = lax.broadcasted_iota(I32, (128, LANES), 1)
    row = lax.broadcasted_iota(I32, (128, LANES), 0)
    own_tile = (lane & 15) == (row & 15)

    def scatter(slab, i, source):
        for t in range(TILES_DEV):
            q = i * TILES_DEV + t
            back[pl.ds(slot_ref[slab * 128 + q], 1), :] = source[q : q + 1, :]

    def backward(slab, behind, target, previous, source):
        pieces = [None] * 8
        for i in range(7, -1, -1):
            at = pl.ds(pl.multiple_of(slab * 128, 128) + i * 16, 16)
            cols = rows[at, COL_OPACITY : COL_OPACITY + 4]
            alpha = alphas[at, :]
            gain = (
                res_red * cols[:, 1:2] + res_green * cols[:, 2:3] + res_blue * cols[:, 3:4]
            ) - behind
            pieces[i] = weights[at, :] * gain
            behind = behind + alpha * gain
            if source is not None:
                scatter(previous, i, source)
        slope = jnp.concatenate(pieces, 0)
        slope_top = slope.astype(BF16)
        slope_rest = (slope - slope_top.astype(F32)).astype(BF16)
        weight = weights[pl.ds(pl.multiple_of(slab * 128, 128), 128), :]
        weight_top = weight.astype(BF16)
        weight_rest = (weight - weight_top.astype(F32)).astype(BF16)
        moment = jnp.dot(slope_top, mono_ref[...], preferred_element_type=F32)
        moment = moment + jnp.dot(slope_rest, mono_ref[...], preferred_element_type=F32)
        both = jnp.dot(weight_top, resid[...], preferred_element_type=F32)
        shade = both[:, :128] + both[:, 128:]
        shade = shade + jnp.dot(weight_rest, resid[:, 0:128], preferred_element_type=F32)
        target[...] = moment + jnp.where(own_tile, shade, 0.0)
        return behind

    behind = backward(SLABS - 1, blank, out_a, None, None)

    def backward_pair(pair, behind):
        slab = SLABS - 2 - 2 * pair
        behind = backward(slab, behind, out_b, slab + 1, out_a)
        return backward(slab - 1, behind, out_a, slab, out_b)

    behind = lax.fori_loop(0, SLABS // 2 - 1, backward_pair, behind, unroll=2)
    backward(0, behind, out_b, 1, out_a)
    for i in range(8):
        scatter(0, i, out_b)

    def finish(o, _):
        turned = back[pl.ds(pl.multiple_of(o * 128, 128), 128), 0:64].T
        for k in range(6):
            moment_ref[k, pl.ds(o, 1), :] = turned[k : k + 1]
        for ch in range(3):
            part = turned[16 + 16 * ch : 32 + 16 * ch]
            moment_ref[6 + ch, pl.ds(o, 1), :] = jnp.sum(part, axis=0, keepdims=True)
        return 0

    lax.fori_loop(0, OWN, finish, 0, unroll=4)


def render(slots, fields, target):
    lines, mono = render_constants()
    vmem = pl.BlockSpec(memory_space=pltpu.VMEM)
    entries = SLABS * 128
    return pl.pallas_call(
        render_kernel,
        out_shape=(
            jax.ShapeDtypeStruct((3, TILES_DEV, PIX), F32),
            jax.ShapeDtypeStruct((FIELDS + 1, OWN, LANES), F32),
        ),
        in_specs=[pl.BlockSpec(memory_space=pltpu.SMEM)] + [vmem] * 4,
        out_specs=(vmem, vmem),
        scratch_shapes=[
            pltpu.VMEM((OWN * LANES, LANES), F32),
            pltpu.VMEM((entries + 256, LANES), F32),
            pltpu.VMEM((entries, PIX), F32),
            pltpu.VMEM((entries, PIX), F32),
            pltpu.VMEM((128, LANES), F32),
            pltpu.VMEM((128, LANES), F32),
            pltpu.VMEM((PIX, 256), BF16),
            pltpu.VMEM((OWN * LANES, LANES), F32),
        ],
        compiler_params=params_of(56),
        name="render",
    )(slots, fields, target, lines, mono)


def adam_update(params, moment_one, second, gradient, step_index):
    step_count = adam_start + step_index + 1
    moment_one = beta_one * moment_one + (1.0 - beta_one) * gradient
    second = beta_two * second + (1.0 - beta_two) * gradient * gradient
    scaled_first = moment_one / (1.0 - beta_one**step_count)
    scaled_second = second / (1.0 - beta_two**step_count)
    params = params - learn_rate * scaled_first / (jnp.sqrt(scaled_second) + adam_eps)
    return (params, moment_one, second)


def per_device(gauss_params, first_moment, second_moment, splat_lists, tile_ids, targets, camera):
    local_count = gauss_params.shape[1]
    params, moment_one, moment_two = (gauss_params, first_moment, second_moment)
    ids = jnp.swapaxes(splat_lists, 1, 2).reshape(STEPS, SLABS, LANES)
    lane_tiles = jnp.tile(tile_ids, (1, LANES // TILES_DEV))
    slots, asked = routing(ids, lane_tiles[:, None, :])
    slots = slots.reshape(STEPS, SLABS * LANES)
    pictures = []
    losses = []
    for step_index in range(STEPS):
        projected, pullback, inverses = jax.vjp(
            lambda values: project(values, camera[step_index]), params, has_aux=True
        )
        table = factor_rows(projected, inverses).reshape(FIELDS, 16, 128)
        fields, shifts = owner_gather(step_index, table, asked)
        target = jnp.swapaxes(targets[step_index], 0, 1)
        picture, moments = render(slots[step_index], fields, target)
        sums, loss = owner_scatter(step_index, moments, shifts, asked)
        sums = sums.reshape(FIELDS, local_count)
        losses.append(loss[0, 0])
        conic_a, conic_b, conic_c = projected[2], projected[3], projected[4]
        cotangent = jnp.concatenate(
            [
                jnp.stack(
                    [
                        conic_a * sums[0] + conic_b * sums[1],
                        conic_b * sums[0] + conic_c * sums[1],
                        -0.5 * sums[2],
                        -sums[3],
                        -0.5 * sums[4],
                    ]
                ),
                sums[5:9],
            ],
            0,
        )
        gradient = pullback(cotangent)[0]
        params, moment_one, moment_two = adam_update(
            params, moment_one, moment_two, gradient, step_index
        )
        pictures.append(jnp.swapaxes(picture, 0, 1))
    loss_values = jnp.stack(losses) / (3.0 * PIX * TILES_DEV * OWN)
    return (params, moment_one, moment_two, jnp.stack(pictures), loss_values)


def solution(mesh):
    both = ("gx", "gy")
    in_specs = (
        P(None, both),
        P(None, both),
        P(None, both),
        P(None, both, None),
        P(None, both),
        P(None, both, None, None),
        P(),
    )
    out_specs = (
        P(None, both),
        P(None, both),
        P(None, both),
        P(None, both, None, None),
        P(),
    )
    return jax.shard_map(
        per_device, mesh=mesh, in_specs=in_specs, out_specs=out_specs, check_vma=False
    )
```

```python
import functools
import math

import jax
import jax.numpy as jnp
import numpy as np
from jax import lax
from jax.experimental import pallas as pl
from jax.experimental.pallas import tpu as pltpu
from jax.sharding import PartitionSpec as P

SIDE = 16
PIX = 256
NCOEF = 16
STEPS = 2
IMG_TX = 64
IMG_TY = 32
OWN = 128
LANES = 128
TILES_DEV = 16
LIST = 512
SLABS = LIST * TILES_DEV // 128
FIELDS = 9
F32 = jnp.float32
BF16 = jnp.bfloat16
I32 = jnp.int32

beta_one = 0.9
beta_two = 0.999
adam_eps = 1e-08
learn_rate = 0.01
adam_start = 1000
band_zero = 0.28209479177387814
band_one = 0.4886025119029199
band_two = (
    1.0925484305920792,
    -1.0925484305920792,
    0.31539156525252005,
    -1.0925484305920792,
    0.5462742152960396,
)
band_three = (
    -0.5900435899266435,
    2.890611442640554,
    -0.4570457994644658,
    0.3731763325901154,
    -0.4570457994644658,
    1.445305721320277,
    -0.5900435899266435,
)
half_log2e = math.sqrt(0.5 * math.log2(math.e))


def params_of(megabytes):
    return pltpu.CompilerParams(vmem_limit_bytes=megabytes << 20)


def harmonics(ray_x, ray_y, ray_z):
    sq_x = ray_x * ray_x
    sq_y = ray_y * ray_y
    sq_z = ray_z * ray_z
    return jnp.stack(
        [
            band_zero * jnp.ones_like(ray_x),
            -band_one * ray_y,
            band_one * ray_z,
            -band_one * ray_x,
            band_two[0] * ray_x * ray_y,
            band_two[1] * ray_y * ray_z,
            band_two[2] * (2.0 * sq_z - sq_x - sq_y),
            band_two[3] * ray_x * ray_z,
            band_two[4] * (sq_x - sq_y),
            band_three[0] * ray_y * (3.0 * sq_x - sq_y),
            band_three[1] * ray_x * ray_y * ray_z,
            band_three[2] * ray_y * (4.0 * sq_z - sq_x - sq_y),
            band_three[3] * ray_z * (2.0 * sq_z - 3.0 * sq_x - 3.0 * sq_y),
            band_three[4] * ray_x * (4.0 * sq_z - sq_x - sq_y),
            band_three[5] * ray_z * (sq_x - sq_y),
            band_three[6] * ray_x * (sq_x - 3.0 * sq_y),
        ]
    )


def project(gauss_rows, camera_row):
    image_width = 1.0 * SIDE * IMG_TX
    image_height = 1.0 * SIDE * IMG_TY
    depth_z = gauss_rows[2]
    screen_u = (gauss_rows[0] - camera_row[0]) / depth_z
    screen_v = (gauss_rows[1] - camera_row[1]) / depth_z
    inv_one = depth_z * depth_z * jnp.exp(-2.0 * gauss_rows[3])
    inv_two = depth_z * depth_z * jnp.exp(-2.0 * gauss_rows[4])
    cosine = jnp.cos(gauss_rows[5])
    sine_angle = jnp.sin(gauss_rows[5])
    conic_a = cosine * cosine * inv_one + sine_angle * sine_angle * inv_two
    conic_b = cosine * sine_angle * (inv_one - inv_two)
    conic_c = sine_angle * sine_angle * inv_one + cosine * cosine * inv_two
    log_opacity = math.log(0.99) - jax.nn.softplus(-gauss_rows[6])
    ray_x = (screen_u - 0.5 * image_width) / image_width
    ray_y = (screen_v - 0.5 * image_height) / image_width
    factor = lax.rsqrt(ray_x * ray_x + ray_y * ray_y + 1.0)
    harmonic_basis = harmonics(ray_x * factor, ray_y * factor, factor)
    coeffs = gauss_rows[7:].reshape(3, NCOEF, gauss_rows.shape[1])
    colour = 0.5 + jnp.sum(coeffs * harmonic_basis[None], axis=1)
    geometry = jnp.stack([screen_u, screen_v, conic_a, conic_b, conic_c, log_opacity])
    return jnp.concatenate([geometry, colour], 0), (inv_one, inv_two)


def factor_rows(projected, inverses):
    conic_a, conic_b, conic_c = projected[2], projected[3], projected[4]
    inv_one, inv_two = inverses
    has_a = conic_a > 0.0
    safe_a = jnp.where(has_a, conic_a, 1.0)
    root = jnp.sqrt(safe_a)
    alpha = jnp.where(has_a, half_log2e * root, 0.0)
    beta = jnp.where(has_a, half_log2e * conic_b / root, 0.0)
    gamma = half_log2e * jnp.where(
        has_a, jnp.sqrt(inv_one * (inv_two / safe_a)), jnp.sqrt(conic_c)
    )
    log2_opacity = jnp.maximum(projected[5] * math.log2(math.e), -1.0e4)
    return jnp.concatenate(
        [projected[0:2], jnp.stack([alpha, beta, gamma, log2_opacity]), projected[6:9]], 0
    )


def split3(values):
    hi = values.astype(BF16).astype(F32)
    rest = values - hi
    mid = rest.astype(BF16).astype(F32)
    return hi, mid, rest - mid


def my_index():
    return lax.axis_index("gx") * lax.axis_size("gy") + lax.axis_index("gy")


def mesh_place(device):
    inner = lax.axis_size("gy")
    return (device // inner, lax.rem(device, inner))


def greet():
    barrier = pltpu.get_barrier_semaphore()
    me = my_index()

    def one(k, _):
        pl.semaphore_signal(
            barrier,
            inc=1,
            device_id=mesh_place(lax.rem(me + k, OWN)),
            device_id_type=pl.DeviceIdType.MESH,
        )
        return 0

    lax.fori_loop(1, OWN, one, 0, unroll=2)


def all_entered():
    pl.semaphore_wait(pltpu.get_barrier_semaphore(), OWN - 1)


def send(source, target, peer, send_sem, recv_sem):
    me = my_index()
    pltpu.make_async_remote_copy(
        src_ref=source.at[:, peer, :],
        dst_ref=target.at[:, me, :],
        send_sem=send_sem,
        recv_sem=recv_sem,
        device_id=mesh_place(peer),
        device_id_type=pl.DeviceIdType.MESH,
    ).start()


def all_but_one(source, target, send_sem, recv_sem):
    blocks = pl.ds(0, OWN - 1)
    return pltpu.make_async_remote_copy(
        src_ref=source.at[:, blocks, :],
        dst_ref=target.at[:, blocks, :],
        send_sem=send_sem,
        recv_sem=recv_sem,
        device_id=mesh_place(my_index()),
        device_id_type=pl.DeviceIdType.MESH,
    )


def keep_own(source, target):
    me = my_index()
    for k in range(source.shape[0]):
        target[k, pl.ds(me, 1), :] = source[k, pl.ds(me, 1), :]


def remote_params(collective_id, megabytes=32):
    return pltpu.CompilerParams(
        collective_id=collective_id, has_side_effects=True, vmem_limit_bytes=megabytes << 20
    )


GROUP = 4


def routing_kernel(ids_ref, tile_ref, upper_ref, slot_ref, asked_ref, request, send_sem, recv_sem):
    greet()
    row_iota = lax.broadcasted_iota(I32, (OWN, LANES), 0)
    own_tile = (lax.broadcasted_iota(I32, (1, LANES), 1) & (TILES_DEV - 1)).astype(F32)
    zero = jnp.zeros((OWN, LANES), F32)
    upper = upper_ref[...]

    def body(k, carry):
        out = []
        for s in range(STEPS):
            counts, acc = carry[s]
            members, cells = [], []
            for c in range(GROUP):
                ids = ids_ref[s, pl.ds(k * GROUP + c, 1), :]
                owner = lax.shift_right_logical(ids, 11)
                member = row_iota == owner
                member_bf = jnp.where(member, 1.0, 0.0).astype(BF16)
                ahead = jnp.dot(member_bf, upper, preferred_element_type=F32)
                rank = jnp.sum(
                    jnp.where(member, ahead[:, :LANES] + counts, 0.0), axis=0, keepdims=True
                ).astype(I32)
                counts = counts + ahead[:, LANES:]
                slot_ref[s, pl.ds(k * GROUP + c, 1), :] = owner * LANES + rank
                here = row_iota == rank
                low = (ids & 127).astype(F32)
                high = (lax.shift_right_logical(ids, 7) & 15).astype(F32) * 16.0 + own_tile
                members.append(member_bf)
                cells.append(
                    jnp.concatenate(
                        [
                            jnp.where(here, low, 0.0).astype(BF16),
                            jnp.where(here, high, 0.0).astype(BF16),
                        ],
                        0,
                    )
                )
            acc = acc + lax.dot_general(
                jnp.concatenate(members, 1),
                jnp.concatenate(cells, 1),
                (((1,), (1,)), ((), ())),
                preferred_element_type=F32,
            )
            out.append((counts, acc))
        return tuple(out)

    start = tuple((zero, jnp.zeros((OWN, 2 * LANES), F32)) for _ in range(STEPS))
    done = lax.fori_loop(0, SLABS // GROUP, body, start)
    for s in range(STEPS):
        acc = done[s][1].astype(I32)
        high = acc[:, LANES:]
        request[s] = acc[:, :LANES] + lax.shift_right_logical(high, 4) * 128
        request[STEPS + s] = jnp.take_along_axis(
            jnp.broadcast_to(tile_ref[s], (OWN, LANES)),
            high & 15,
            axis=1,
            mode="promise_in_bounds",
        )
    all_entered()
    me = my_index()

    def push(k, _):
        send(request, asked_ref, lax.rem(me + k, OWN), send_sem, recv_sem)
        return 0

    lax.fori_loop(1, OWN, push, 0, unroll=2)
    keep_own(request, asked_ref)
    rest = all_but_one(request, asked_ref, send_sem, recv_sem)
    rest.wait_send()
    rest.wait_recv()


def routing(ids, lane_tiles):
    strict = np.triu(np.ones((128, 128), np.float32), 1)
    upper = jnp.asarray(np.concatenate([strict, np.ones((128, 128), np.float32)], 1), BF16)
    vmem = pl.BlockSpec(memory_space=pltpu.VMEM)
    return pl.pallas_call(
        routing_kernel,
        out_shape=(
            jax.ShapeDtypeStruct((STEPS, SLABS, LANES), I32),
            jax.ShapeDtypeStruct((2 * STEPS, OWN, LANES), I32),
        ),
        in_specs=[vmem] * 3,
        out_specs=(vmem, vmem),
        scratch_shapes=[
            pltpu.VMEM((2 * STEPS, OWN, LANES), I32),
            pltpu.SemaphoreType.DMA,
            pltpu.SemaphoreType.DMA,
        ],
        compiler_params=remote_params(0),
        name="routing",
    )(ids, lane_tiles, upper)


BLOCKS = 8


def gather_kernel(
    step, table_ref, asked_ref, out_ref, shift_ref, parts, got, answer, send_sem, recv_sem
):
    greet()
    for f in range(FIELDS):
        for p, part in enumerate(split3(table_ref[f])):
            parts[f * 16 : f * 16 + 16, p * 128 : p * 128 + 128] = part.astype(BF16)
    low_iota = lax.broadcasted_iota(I32, (128, 256), 0)
    high_iota = lax.broadcasted_iota(I32, (16, 256), 0)
    me = my_index()
    groups = OWN // BLOCKS

    def group_of(k):
        return lax.rem(me // BLOCKS + k, groups)

    def compute(group):
        first = pl.multiple_of(group * BLOCKS, BLOCKS)
        for pair in range(BLOCKS // 2):
            d = first + 2 * pair
            want = jnp.concatenate(
                [asked_ref[step, pl.ds(d, 1), :], asked_ref[step, pl.ds(d + 1, 1), :]], 1
            )
            hot = jnp.where(low_iota == (want & 127), 1.0, 0.0).astype(BF16)
            hot = jnp.concatenate([hot, hot, hot], 0)
            here = high_iota == lax.shift_right_logical(want, 7)
            picked = jnp.dot(parts[...], hot, preferred_element_type=F32)
            for f in range(FIELDS):
                row = jnp.sum(
                    jnp.where(here, picked[f * 16 : f * 16 + 16], 0.0), axis=0, keepdims=True
                )
                got[f, 2 * pair : 2 * pair + 1, :] = row[:, :128]
                got[f, 2 * pair + 1 : 2 * pair + 2, :] = row[:, 128:]
        at = pl.ds(first, BLOCKS)
        tile = asked_ref[STEPS + step, at, :]
        centre_x = ((tile & (IMG_TX - 1)) * SIDE + SIDE // 2).astype(F32)
        centre_y = (lax.shift_right_logical(tile, 6) * SIDE + SIDE // 2).astype(F32)
        local_u = got[0] - centre_x
        local_v = got[1] - centre_y
        shift_ref[0, at, :] = local_u
        shift_ref[1, at, :] = local_v
        alpha, beta, gamma = got[2], got[3], got[4]
        answer[0, at, :] = alpha
        answer[1, at, :] = beta
        answer[2, at, :] = gamma
        answer[3, at, :] = -(alpha * local_u + beta * local_v)
        answer[4, at, :] = -gamma * local_v
        for f in range(5, FIELDS):
            answer[f, at, :] = got[f]

    def push(group):
        for k in range(BLOCKS):
            peer = group * BLOCKS + lax.rem(me + k, BLOCKS)
            send(answer, out_ref, peer, send_sem, recv_sem)

    def early(k, _):
        compute(group_of(k))
        return 0

    half = groups // 2
    lax.fori_loop(0, half, early, 0)
    all_entered()

    def late(k, _):
        push(group_of(2 * k + 1))
        push(group_of(2 * k + 2))
        compute(group_of(k + half))
        return 0

    lax.fori_loop(0, half - 2, late, 0)
    compute(group_of(groups - 2))
    push(group_of(groups - 3))
    compute(group_of(groups - 1))
    push(group_of(groups - 2))
    push(group_of(groups - 1))

    def inside(k, _):
        send(answer, out_ref, me // BLOCKS * BLOCKS + lax.rem(me + k, BLOCKS), send_sem, recv_sem)
        return 0

    lax.fori_loop(1, BLOCKS, inside, 0)
    keep_own(answer, out_ref)
    rest = all_but_one(answer, out_ref, send_sem, recv_sem)
    rest.wait_send()
    rest.wait_recv()


def owner_gather(step, table, asked):
    vmem = pl.BlockSpec(memory_space=pltpu.VMEM)
    return pl.pallas_call(
        functools.partial(gather_kernel, step),
        out_shape=(
            jax.ShapeDtypeStruct((FIELDS, OWN, LANES), F32),
            jax.ShapeDtypeStruct((2, OWN, LANES), F32),
        ),
        in_specs=[vmem] * 2,
        out_specs=(vmem, vmem),
        scratch_shapes=[
            pltpu.VMEM((FIELDS * 16, 384), BF16),
            pltpu.VMEM((FIELDS, BLOCKS, LANES), F32),
            pltpu.VMEM((FIELDS, OWN, LANES), F32),
            pltpu.SemaphoreType.DMA,
            pltpu.SemaphoreType.DMA,
        ],
        compiler_params=remote_params(1 + step),
        name="owner_gather",
    )(table, asked)


def scatter_kernel(
    step, moment_ref, shift_ref, asked_ref, out_ref, loss_ref,
    arrived, high, rest, own_sem, send_sem, recv_sems,
):
    greet()
    me = my_index()
    groups = OWN // BLOCKS
    mine = me // BLOCKS
    all_entered()

    def push(k, _):
        send(moment_ref, arrived, lax.rem(me + k, OWN), send_sem, recv_sems.at[mine])
        return 0

    lax.fori_loop(1, OWN, push, 0, unroll=2)
    own = pltpu.make_async_copy(moment_ref.at[:, me, :], arrived.at[:, me, :], own_sem)
    own.start()
    own.wait()
    low_iota = lax.broadcasted_iota(I32, (128, 128), 0)
    high_iota = lax.broadcasted_iota(I32, (16, 128), 0)

    def landed(group, count):
        blocks = pl.ds(group * BLOCKS, count)
        pltpu.make_async_remote_copy(
            src_ref=moment_ref.at[:, blocks, :],
            dst_ref=arrived.at[:, blocks, :],
            send_sem=send_sem,
            recv_sem=recv_sems.at[group],
            device_id=mesh_place(me),
            device_id_type=pl.DeviceIdType.MESH,
        ).wait_recv()

    def body(k, carry):
        acc, loss = carry
        group = lax.rem(mine + groups - k, groups)

        @pl.when(k == 0)
        def _():
            landed(group, BLOCKS - 1)

        @pl.when(k != 0)
        def _():
            landed(group, BLOCKS)

        first = pl.multiple_of(group * BLOCKS, BLOCKS)
        at = pl.ds(first, BLOCKS)
        local_u, local_v = shift_ref[0, at, :], shift_ref[1, at, :]
        m0, mx, my = arrived[0, at, :], arrived[1, at, :], arrived[2, at, :]
        sx = mx - local_u * m0
        sy = my - local_v * m0
        sums = [
            sx,
            sy,
            arrived[3, at, :] - local_u * (mx + sx),
            arrived[4, at, :] - local_u * my - local_v * sx,
            arrived[5, at, :] - local_v * (my + sy),
            m0,
            arrived[6, at, :],
            arrived[7, at, :],
            arrived[8, at, :],
        ]
        for f in range(FIELDS):
            top = sums[f].astype(BF16).astype(F32)
            high[f] = top
            rest[f] = sums[f] - top
        for pair in range(BLOCKS // 2):
            lefts, rights = [], []
            for half in range(2):
                d = 2 * pair + half
                want = asked_ref[step, pl.ds(first + d, 1), :]
                rights.append(jnp.where(low_iota == (want & 127), 1.0, 0.0).astype(BF16))
                here = high_iota == lax.shift_right_logical(want, 7)
                rows = [
                    jnp.where(here, ref[f, d : d + 1, :], 0.0).astype(BF16)
                    for ref in (high, rest)
                    for f in range(FIELDS)
                ]
                lefts.append(jnp.concatenate(rows, 0))
            acc = acc + lax.dot_general(
                jnp.concatenate(lefts, 1),
                jnp.concatenate(rights, 1),
                (((1,), (1,)), ((), ())),
                preferred_element_type=F32,
            )
        return acc, loss + arrived[FIELDS, at, :]

    acc, loss = lax.fori_loop(
        0,
        groups,
        body,
        (jnp.zeros((2 * FIELDS * 16, 128), F32), jnp.zeros((BLOCKS, LANES), F32)),
    )
    out_ref[...] = acc[: FIELDS * 16] + acc[FIELDS * 16 :]
    loss_ref[...] = jnp.sum(loss, axis=0, keepdims=True)
    all_but_one(moment_ref, arrived, send_sem, own_sem).wait_send()


def owner_scatter(step, moments, shifts, asked):
    vmem = pl.BlockSpec(memory_space=pltpu.VMEM)
    return pl.pallas_call(
        functools.partial(scatter_kernel, step),
        out_shape=(
            jax.ShapeDtypeStruct((FIELDS * 16, 128), F32),
            jax.ShapeDtypeStruct((1, LANES), F32),
        ),
        in_specs=[vmem] * 3,
        out_specs=(vmem, vmem),
        scratch_shapes=[
            pltpu.VMEM((FIELDS + 1, OWN, LANES), F32),
            pltpu.VMEM((FIELDS, BLOCKS, LANES), F32),
            pltpu.VMEM((FIELDS, BLOCKS, LANES), F32),
            pltpu.SemaphoreType.DMA,
            pltpu.SemaphoreType.DMA,
            pltpu.SemaphoreType.DMA((OWN // BLOCKS,)),
        ],
        compiler_params=remote_params(1 + STEPS + step),
        name="owner_scatter",
    )(moments, shifts, asked)


PACK = 8


def render_constants():
    axis = np.arange(SIDE, dtype=np.float32) - 7.5
    x = np.tile(axis, SIDE)
    y = np.repeat(axis, SIDE)
    one = np.ones_like(x)
    zero = np.zeros_like(x)
    block = np.zeros((8, 512), np.float32)
    block[0] = np.concatenate([x, zero])
    block[1] = np.concatenate([y, zero])
    block[2] = np.concatenate([zero, y])
    block[3] = np.concatenate([one, zero])
    block[4] = np.concatenate([zero, one])
    lines = np.concatenate([block, block, block, np.zeros_like(block)], 0)
    mono = np.zeros((2 * PIX, 128), np.float32)
    for k, column in enumerate((one, x, y, x * x, x * y, y * y)):
        mono[:, k * PACK : (k + 1) * PACK] = np.tile(column, 2)[:, None]
    fold = np.zeros((256, 128), np.float32)
    for ch in range(3):
        for half in range(2):
            at = half * 128 + ch * TILES_DEV
            fold[at : at + TILES_DEV, (6 + ch) * PACK : (7 + ch) * PACK] = 1.0
    return jnp.asarray(lines, BF16), jnp.asarray(mono, BF16), jnp.asarray(fold, BF16)


BATCH = 2
COL_OPACITY = 29


def split2(values):
    high = values.astype(BF16)
    return high, (values - high.astype(F32)).astype(BF16)


def render_kernel(
    slot_ref, fields_ref, target_ref, lines_ref, mono_ref, fold_ref,
    picture_ref, moment_ref,
    table, rows, alphas, weights, out_ref, resid, back,
):
    def build(o, _):
        first = fields_ref[0:8, pl.ds(o, 1), :].reshape(8, LANES)
        last = jnp.broadcast_to(fields_ref[8, pl.ds(o, 1), :], (8, LANES))
        stack = jnp.concatenate([*split3(first), first, last], 0)
        table[pl.ds(pl.multiple_of(o * 128, 128), 128), 0:40] = stack.T
        return 0

    lax.fori_loop(0, OWN, build, 0, unroll=4)

    sublane = lax.broadcasted_iota(I32, (8, LANES), 0)

    def fetch(slab, i):
        source = jnp.minimum(slab, SLABS - 1) * 128 + i * TILES_DEV
        for half in range(0, TILES_DEV, 8):
            got = None
            for t in range(8):
                row = table[pl.ds(slot_ref[source + half + t], 1), :]
                row = jnp.broadcast_to(row, (8, LANES))
                got = row if t == 0 else jnp.where(sublane == t, row, got)
            at = pl.multiple_of(slab * 128, 128) + i * TILES_DEV + half
            rows[pl.ds(at, 8), :] = got

    def forward(slab, state):
        through, red, green, blue = state
        for i in range(8):
            at = pl.ds(pl.multiple_of(slab * 128, 128) + i * 16, 16)
            both = jnp.dot(
                rows[at, 0:32].astype(BF16), lines_ref[...], preferred_element_type=F32
            )
            first = both[:, 0:256]
            second = both[:, 256:512]
            cols = rows[at, COL_OPACITY : COL_OPACITY + 4]
            alpha = jnp.exp2(cols[:, 0:1] - first * first - second * second)
            weight = through * alpha
            through = through - weight
            red = red + weight * cols[:, 1:2]
            green = green + weight * cols[:, 2:3]
            blue = blue + weight * cols[:, 3:4]
            alphas[at, :] = alpha
            weights[at, :] = weight
            back[pl.ds(pl.multiple_of(slab * 256, 256) + i * 32, 32), :] = jnp.zeros(
                (32, LANES), F32
            )
            fetch(slab + 1, i)
        return through, red, green, blue

    for i in range(8):
        fetch(0, i)
    blank = jnp.zeros((TILES_DEV, PIX), F32)
    _, red, green, blue = lax.fori_loop(
        0,
        SLABS,
        forward,
        (jnp.ones((TILES_DEV, PIX), F32), blank, blank, blank),
        unroll=4,
    )
    residuals = []
    total = jnp.zeros((), F32)
    for ch, colour in enumerate((red, green, blue)):
        picture_ref[ch] = colour
        residual = colour - target_ref[ch]
        residuals.append(residual)
        total = total + jnp.sum(residual * residual)
    moment_ref[FIELDS] = jnp.full((OWN, LANES), 0.5 * total, F32)
    res_red, res_green, res_blue = residuals

    padded = jnp.concatenate([*residuals, jnp.zeros((80, PIX), F32)], 0)
    turned = padded.T
    top = turned.astype(BF16)
    resid[:, 0:128] = top
    resid[:, 128:256] = (turned - top.astype(F32)).astype(BF16)

    lane = lax.broadcasted_iota(I32, (128, LANES), 1)
    row = lax.broadcasted_iota(I32, (128, LANES), 0)
    own_tile = (lane & 15) == (row & 15)

    def scatter(slab, i, source, base):
        for t in range(TILES_DEV):
            q = i * TILES_DEV + t
            back[pl.ds(slot_ref[slab * 128 + q], 1), :] = source[base + q : base + q + 1, :]

    own_rows = jnp.concatenate([own_tile] * BATCH, 0)

    def backward(turn, behind, target, previous, source):
        first = pl.multiple_of(turn * (BATCH * 128), BATCH * 128)
        every = pl.ds(first, BATCH * 128)
        weight_top, weight_rest = split2(weights[every, :])
        both = jnp.dot(weight_top, resid[...], preferred_element_type=F32)
        shade = both[:, :128] + both[:, 128:]
        shade = shade + jnp.dot(weight_rest, resid[:, 0:128], preferred_element_type=F32)
        shade = jnp.concatenate(split2(jnp.where(own_rows, shade, 0.0)), 1)
        pieces = [None] * (8 * BATCH)
        for i in range(8 * BATCH - 1, -1, -1):
            at = pl.ds(first + i * 16, 16)
            cols = rows[at, COL_OPACITY : COL_OPACITY + 4]
            gain = (
                res_red * cols[:, 1:2] + res_green * cols[:, 2:3] + res_blue * cols[:, 3:4]
            ) - behind
            pieces[i] = weights[at, :] * gain
            behind = behind + alphas[at, :] * gain
            if source is not None:
                scatter(previous * BATCH + i // 8, i % 8, source, i // 8 * 128)
        slope = jnp.concatenate(split2(jnp.concatenate(pieces, 0)), 1)
        target[...] = jnp.dot(slope, mono_ref[...], preferred_element_type=F32) + jnp.dot(
            shade, fold_ref[...], preferred_element_type=F32
        )
        return behind

    batches = SLABS // BATCH
    outs = [out_ref.at[k] for k in range(2)]
    behind = backward(batches - 1, blank, outs[1], None, None)

    def backward_two(k, behind):
        turn = batches - 2 - 2 * k
        behind = backward(turn, behind, outs[0], turn + 1, outs[1])
        return backward(turn - 1, behind, outs[1], turn, outs[0])

    behind = lax.fori_loop(0, batches // 2 - 1, backward_two, behind)
    backward(0, behind, outs[0], 1, outs[1])
    for i in range(8 * BATCH):
        scatter(i // 8, i % 8, outs[0], i // 8 * 128)

    turn = lax.broadcasted_iota(I32, (128, LANES), 1) & (PACK - 1)
    for g in range(OWN // PACK):
        merged = back[g * 1024 : g * 1024 + 128, :]
        for k in range(1, PACK):
            at = g * 1024 + k * 128
            merged = jnp.where(turn == k, back[at : at + 128, :], merged)
        merged = merged.T
        for f in range(FIELDS):
            moment_ref[f, g * PACK : (g + 1) * PACK, :] = merged[f * PACK : (f + 1) * PACK]


def render(slots, fields, target):
    constants = render_constants()
    vmem = pl.BlockSpec(memory_space=pltpu.VMEM)
    entries = SLABS * 128
    return pl.pallas_call(
        render_kernel,
        out_shape=(
            jax.ShapeDtypeStruct((3, TILES_DEV, PIX), F32),
            jax.ShapeDtypeStruct((FIELDS + 1, OWN, LANES), F32),
        ),
        in_specs=[pl.BlockSpec(memory_space=pltpu.SMEM)] + [vmem] * 5,
        out_specs=(vmem, vmem),
        scratch_shapes=[
            pltpu.VMEM((OWN * LANES, LANES), F32),
            pltpu.VMEM((entries + 256, LANES), F32),
            pltpu.VMEM((entries, PIX), F32),
            pltpu.VMEM((entries, PIX), F32),
            pltpu.VMEM((2, BATCH * 128, LANES), F32),
            pltpu.VMEM((PIX, 256), BF16),
            pltpu.VMEM((OWN * LANES, LANES), F32),
        ],
        compiler_params=params_of(56),
        name="render",
    )(slots, fields, target, *constants)


def adam_update(params, moment_one, second, gradient, step_index):
    step_count = adam_start + step_index + 1
    moment_one = beta_one * moment_one + (1.0 - beta_one) * gradient
    second = beta_two * second + (1.0 - beta_two) * gradient * gradient
    scaled_first = moment_one / (1.0 - beta_one**step_count)
    scaled_second = second / (1.0 - beta_two**step_count)
    params = params - learn_rate * scaled_first / (jnp.sqrt(scaled_second) + adam_eps)
    return (params, moment_one, second)


def per_device(gauss_params, first_moment, second_moment, splat_lists, tile_ids, targets, camera):
    local_count = gauss_params.shape[1]
    params, moment_one, moment_two = (gauss_params, first_moment, second_moment)
    ids = jnp.swapaxes(splat_lists, 1, 2).reshape(STEPS, SLABS, LANES)
    lane_tiles = jnp.tile(tile_ids, (1, LANES // TILES_DEV))
    slots, asked = routing(ids, lane_tiles[:, None, :])
    slots = slots.reshape(STEPS, SLABS * LANES)
    pictures = []
    losses = []
    for step_index in range(STEPS):
        projected, pullback, inverses = jax.vjp(
            lambda values: project(values, camera[step_index]), params, has_aux=True
        )
        table = factor_rows(projected, inverses).reshape(FIELDS, 16, 128)
        fields, shifts = owner_gather(step_index, table, asked)
        target = jnp.swapaxes(targets[step_index], 0, 1)
        picture, moments = render(slots[step_index], fields, target)
        sums, loss = owner_scatter(step_index, moments, shifts, asked)
        sums = sums.reshape(FIELDS, local_count)
        losses.append(loss[0, 0])
        conic_a, conic_b, conic_c = projected[2], projected[3], projected[4]
        cotangent = jnp.concatenate(
            [
                jnp.stack(
                    [
                        conic_a * sums[0] + conic_b * sums[1],
                        conic_b * sums[0] + conic_c * sums[1],
                        -0.5 * sums[2],
                        -sums[3],
                        -0.5 * sums[4],
                    ]
                ),
                sums[5:9],
            ],
            0,
        )
        gradient = pullback(cotangent)[0]
        params, moment_one, moment_two = adam_update(
            params, moment_one, moment_two, gradient, step_index
        )
        pictures.append(jnp.swapaxes(picture, 0, 1))
    loss_values = jnp.stack(losses) / (3.0 * PIX * TILES_DEV * OWN)
    return (params, moment_one, moment_two, jnp.stack(pictures), loss_values)


def solution(mesh):
    both = ("gx", "gy")
    in_specs = (
        P(None, both),
        P(None, both),
        P(None, both),
        P(None, both, None),
        P(None, both),
        P(None, both, None, None),
        P(),
    )
    out_specs = (
        P(None, both),
        P(None, both),
        P(None, both),
        P(None, both, None, None),
        P(),
    )
    return jax.shard_map(
        per_device, mesh=mesh, in_specs=in_specs, out_specs=out_specs, check_vma=False
    )
```

```python
import functools
import math

import jax
import jax.numpy as jnp
import numpy as np
from jax import lax
from jax.experimental import pallas as pl
from jax.experimental.pallas import tpu as pltpu
from jax.sharding import PartitionSpec as P

SIDE = 16
PIX = 256
NCOEF = 16
STEPS = 2
IMG_TX = 64
IMG_TY = 32
OWN = 128
LANES = 128
TILES_DEV = 16
LIST = 512
SLABS = LIST * TILES_DEV // 128
FIELDS = 9
F32 = jnp.float32
BF16 = jnp.bfloat16
I32 = jnp.int32

beta_one = 0.9
beta_two = 0.999
adam_eps = 1e-08
learn_rate = 0.01
adam_start = 1000
band_zero = 0.28209479177387814
band_one = 0.4886025119029199
band_two = (
    1.0925484305920792,
    -1.0925484305920792,
    0.31539156525252005,
    -1.0925484305920792,
    0.5462742152960396,
)
band_three = (
    -0.5900435899266435,
    2.890611442640554,
    -0.4570457994644658,
    0.3731763325901154,
    -0.4570457994644658,
    1.445305721320277,
    -0.5900435899266435,
)
half_log2e = math.sqrt(0.5 * math.log2(math.e))


def params_of(megabytes):
    return pltpu.CompilerParams(vmem_limit_bytes=megabytes << 20)


def harmonics(ray_x, ray_y, ray_z):
    sq_x = ray_x * ray_x
    sq_y = ray_y * ray_y
    sq_z = ray_z * ray_z
    return jnp.stack(
        [
            band_zero * jnp.ones_like(ray_x),
            -band_one * ray_y,
            band_one * ray_z,
            -band_one * ray_x,
            band_two[0] * ray_x * ray_y,
            band_two[1] * ray_y * ray_z,
            band_two[2] * (2.0 * sq_z - sq_x - sq_y),
            band_two[3] * ray_x * ray_z,
            band_two[4] * (sq_x - sq_y),
            band_three[0] * ray_y * (3.0 * sq_x - sq_y),
            band_three[1] * ray_x * ray_y * ray_z,
            band_three[2] * ray_y * (4.0 * sq_z - sq_x - sq_y),
            band_three[3] * ray_z * (2.0 * sq_z - 3.0 * sq_x - 3.0 * sq_y),
            band_three[4] * ray_x * (4.0 * sq_z - sq_x - sq_y),
            band_three[5] * ray_z * (sq_x - sq_y),
            band_three[6] * ray_x * (sq_x - 3.0 * sq_y),
        ]
    )


def project(gauss_rows, camera_row):
    image_width = 1.0 * SIDE * IMG_TX
    image_height = 1.0 * SIDE * IMG_TY
    depth_z = gauss_rows[2]
    screen_u = (gauss_rows[0] - camera_row[0]) / depth_z
    screen_v = (gauss_rows[1] - camera_row[1]) / depth_z
    inv_one = depth_z * depth_z * jnp.exp(-2.0 * gauss_rows[3])
    inv_two = depth_z * depth_z * jnp.exp(-2.0 * gauss_rows[4])
    cosine = jnp.cos(gauss_rows[5])
    sine_angle = jnp.sin(gauss_rows[5])
    conic_a = cosine * cosine * inv_one + sine_angle * sine_angle * inv_two
    conic_b = cosine * sine_angle * (inv_one - inv_two)
    conic_c = sine_angle * sine_angle * inv_one + cosine * cosine * inv_two
    log_opacity = math.log(0.99) - jax.nn.softplus(-gauss_rows[6])
    ray_x = (screen_u - 0.5 * image_width) / image_width
    ray_y = (screen_v - 0.5 * image_height) / image_width
    factor = lax.rsqrt(ray_x * ray_x + ray_y * ray_y + 1.0)
    harmonic_basis = harmonics(ray_x * factor, ray_y * factor, factor)
    coeffs = gauss_rows[7:].reshape(3, NCOEF, gauss_rows.shape[1])
    colour = 0.5 + jnp.sum(coeffs * harmonic_basis[None], axis=1)
    geometry = jnp.stack([screen_u, screen_v, conic_a, conic_b, conic_c, log_opacity])
    return jnp.concatenate([geometry, colour], 0), (inv_one, inv_two)


def factor_rows(projected, inverses):
    conic_a, conic_b, conic_c = projected[2], projected[3], projected[4]
    inv_one, inv_two = inverses
    has_a = conic_a > 0.0
    safe_a = jnp.where(has_a, conic_a, 1.0)
    root = jnp.sqrt(safe_a)
    alpha = jnp.where(has_a, half_log2e * root, 0.0)
    beta = jnp.where(has_a, half_log2e * conic_b / root, 0.0)
    gamma = half_log2e * jnp.where(
        has_a, jnp.sqrt(inv_one * (inv_two / safe_a)), jnp.sqrt(conic_c)
    )
    log2_opacity = jnp.maximum(projected[5] * math.log2(math.e), -1.0e4)
    return jnp.concatenate(
        [projected[0:2], jnp.stack([alpha, beta, gamma, log2_opacity]), projected[6:9]], 0
    )


def split3(values):
    hi = values.astype(BF16).astype(F32)
    rest = values - hi
    mid = rest.astype(BF16).astype(F32)
    return hi, mid, rest - mid


def my_index():
    return lax.axis_index("gx") * lax.axis_size("gy") + lax.axis_index("gy")


def mesh_place(device):
    inner = lax.axis_size("gy")
    return (device // inner, lax.rem(device, inner))


def greet_one(k):
    pl.semaphore_signal(
        pltpu.get_barrier_semaphore(),
        inc=1,
        device_id=mesh_place(lax.rem(my_index() + k, OWN)),
        device_id_type=pl.DeviceIdType.MESH,
    )


def greet(first=1):
    def one(k, _):
        greet_one(k)
        return 0

    lax.fori_loop(first, OWN, one, 0)


def all_entered():
    pl.semaphore_wait(pltpu.get_barrier_semaphore(), OWN - 1)


def send(source, target, peer, send_sem, recv_sem):
    me = my_index()
    pltpu.make_async_remote_copy(
        src_ref=source.at[:, peer, :],
        dst_ref=target.at[:, me, :],
        send_sem=send_sem,
        recv_sem=recv_sem,
        device_id=mesh_place(peer),
        device_id_type=pl.DeviceIdType.MESH,
    ).start()


def all_but_one(source, target, send_sem, recv_sem):
    blocks = pl.ds(0, OWN - 1)
    return pltpu.make_async_remote_copy(
        src_ref=source.at[:, blocks, :],
        dst_ref=target.at[:, blocks, :],
        send_sem=send_sem,
        recv_sem=recv_sem,
        device_id=mesh_place(my_index()),
        device_id_type=pl.DeviceIdType.MESH,
    )


def keep_own(source, target):
    me = my_index()
    for k in range(source.shape[0]):
        target[k, pl.ds(me, 1), :] = source[k, pl.ds(me, 1), :]


def remote_params(collective_id, megabytes=32):
    return pltpu.CompilerParams(
        collective_id=collective_id, has_side_effects=True, vmem_limit_bytes=megabytes << 20
    )


GROUP = 4


def routing_kernel(ids_ref, tile_ref, upper_ref, slot_ref, asked_ref, request, send_sem, recv_sem):
    turns = SLABS // GROUP
    told = (OWN - 1) // turns
    greet(turns * told + 1)
    row_iota = lax.broadcasted_iota(I32, (OWN, LANES), 0)
    own_tile = (lax.broadcasted_iota(I32, (1, LANES), 1) & (TILES_DEV - 1)).astype(F32)
    zero = jnp.zeros((OWN, LANES), F32)
    upper = upper_ref[...]

    def body(k, carry):
        out = []
        for j in range(told):
            greet_one(k * told + 1 + j)
        for s in range(STEPS):
            counts, acc = carry[s]
            members, cells = [], []
            for c in range(GROUP):
                ids = ids_ref[s, pl.ds(k * GROUP + c, 1), :]
                owner = lax.shift_right_logical(ids, 11)
                member = row_iota == owner
                member_bf = jnp.where(member, 1.0, 0.0).astype(BF16)
                ahead = jnp.dot(member_bf, upper, preferred_element_type=F32)
                rank = jnp.sum(
                    jnp.where(member, ahead[:, :LANES] + counts, 0.0), axis=0, keepdims=True
                ).astype(I32)
                counts = counts + ahead[:, LANES:]
                slot_ref[s, pl.ds(k * GROUP + c, 1), :] = owner * LANES + rank
                here = row_iota == rank
                low = (ids & 127).astype(F32)
                high = (lax.shift_right_logical(ids, 7) & 15).astype(F32) * 16.0 + own_tile
                members.append(member_bf)
                cells.append(
                    jnp.concatenate(
                        [
                            jnp.where(here, low, 0.0).astype(BF16),
                            jnp.where(here, high, 0.0).astype(BF16),
                        ],
                        0,
                    )
                )
            acc = acc + lax.dot_general(
                jnp.concatenate(members, 1),
                jnp.concatenate(cells, 1),
                (((1,), (1,)), ((), ())),
                preferred_element_type=F32,
            )
            out.append((counts, acc))
        return tuple(out)

    start = tuple((zero, jnp.zeros((OWN, 2 * LANES), F32)) for _ in range(STEPS))
    done = lax.fori_loop(0, turns, body, start)
    for s in range(STEPS):
        acc = done[s][1].astype(I32)
        high = acc[:, LANES:]
        request[s] = acc[:, :LANES] + lax.shift_right_logical(high, 4) * 128
        request[STEPS + s] = jnp.take_along_axis(
            jnp.broadcast_to(tile_ref[s], (OWN, LANES)),
            high & 15,
            axis=1,
            mode="promise_in_bounds",
        )
    all_entered()
    me = my_index()

    def push(k, _):
        send(request, asked_ref, lax.rem(me + k, OWN), send_sem, recv_sem)
        return 0

    lax.fori_loop(1, OWN, push, 0, unroll=2)
    keep_own(request, asked_ref)
    rest = all_but_one(request, asked_ref, send_sem, recv_sem)
    rest.wait_send()
    rest.wait_recv()


def routing(ids, lane_tiles):
    strict = np.triu(np.ones((128, 128), np.float32), 1)
    upper = jnp.asarray(np.concatenate([strict, np.ones((128, 128), np.float32)], 1), BF16)
    vmem = pl.BlockSpec(memory_space=pltpu.VMEM)
    return pl.pallas_call(
        routing_kernel,
        out_shape=(
            jax.ShapeDtypeStruct((STEPS, SLABS, LANES), I32),
            jax.ShapeDtypeStruct((2 * STEPS, OWN, LANES), I32),
        ),
        in_specs=[vmem] * 3,
        out_specs=(vmem, vmem),
        scratch_shapes=[
            pltpu.VMEM((2 * STEPS, OWN, LANES), I32),
            pltpu.SemaphoreType.DMA,
            pltpu.SemaphoreType.DMA,
        ],
        compiler_params=remote_params(0),
        name="routing",
    )(ids, lane_tiles, upper)


BLOCKS = 8


def gather_kernel(
    step, table_ref, asked_ref, out_ref, shift_ref, parts, got, answer, send_sem, recv_sem
):
    groups = OWN // BLOCKS
    half = groups // 2
    told = (OWN - 1) // half
    greet(half * told + 1)
    for f in range(FIELDS):
        for p, part in enumerate(split3(table_ref[f])):
            parts[f * 16 : f * 16 + 16, p * 128 : p * 128 + 128] = part.astype(BF16)
    low_iota = lax.broadcasted_iota(I32, (128, 256), 0)
    high_iota = lax.broadcasted_iota(I32, (16, 256), 0)
    me = my_index()

    def group_of(k):
        return lax.rem(me // BLOCKS + k, groups)

    def compute(group):
        first = pl.multiple_of(group * BLOCKS, BLOCKS)
        for pair in range(BLOCKS // 2):
            d = first + 2 * pair
            want = jnp.concatenate(
                [asked_ref[step, pl.ds(d, 1), :], asked_ref[step, pl.ds(d + 1, 1), :]], 1
            )
            hot = jnp.where(low_iota == (want & 127), 1.0, 0.0).astype(BF16)
            hot = jnp.concatenate([hot, hot, hot], 0)
            here = high_iota == lax.shift_right_logical(want, 7)
            picked = jnp.dot(parts[...], hot, preferred_element_type=F32)
            for f in range(FIELDS):
                row = jnp.sum(
                    jnp.where(here, picked[f * 16 : f * 16 + 16], 0.0), axis=0, keepdims=True
                )
                got[f, 2 * pair : 2 * pair + 1, :] = row[:, :128]
                got[f, 2 * pair + 1 : 2 * pair + 2, :] = row[:, 128:]
        at = pl.ds(first, BLOCKS)
        tile = asked_ref[STEPS + step, at, :]
        centre_x = ((tile & (IMG_TX - 1)) * SIDE + SIDE // 2).astype(F32)
        centre_y = (lax.shift_right_logical(tile, 6) * SIDE + SIDE // 2).astype(F32)
        local_u = got[0] - centre_x
        local_v = got[1] - centre_y
        shift_ref[0, at, :] = local_u
        shift_ref[1, at, :] = local_v
        alpha, beta, gamma = got[2], got[3], got[4]
        answer[0, at, :] = alpha
        answer[1, at, :] = beta
        answer[2, at, :] = gamma
        answer[3, at, :] = -(alpha * local_u + beta * local_v)
        answer[4, at, :] = -gamma * local_v
        for f in range(5, FIELDS):
            answer[f, at, :] = got[f]

    def push(group):
        for k in range(BLOCKS):
            peer = group * BLOCKS + lax.rem(me + k, BLOCKS)
            send(answer, out_ref, peer, send_sem, recv_sem)

    def early(k, _):
        for j in range(told):
            greet_one(k * told + 1 + j)
        compute(group_of(k))
        return 0

    lax.fori_loop(0, half, early, 0)
    all_entered()

    def late(k, _):
        push(group_of(2 * k + 1))
        push(group_of(2 * k + 2))
        compute(group_of(k + half))
        return 0

    lax.fori_loop(0, half - 2, late, 0)
    compute(group_of(groups - 2))
    push(group_of(groups - 3))
    compute(group_of(groups - 1))
    push(group_of(groups - 2))
    push(group_of(groups - 1))

    def inside(k, _):
        send(answer, out_ref, me // BLOCKS * BLOCKS + lax.rem(me + k, BLOCKS), send_sem, recv_sem)
        return 0

    lax.fori_loop(1, BLOCKS, inside, 0)
    keep_own(answer, out_ref)
    rest = all_but_one(answer, out_ref, send_sem, recv_sem)
    rest.wait_send()
    rest.wait_recv()


def owner_gather(step, table, asked):
    vmem = pl.BlockSpec(memory_space=pltpu.VMEM)
    return pl.pallas_call(
        functools.partial(gather_kernel, step),
        out_shape=(
            jax.ShapeDtypeStruct((FIELDS, OWN, LANES), F32),
            jax.ShapeDtypeStruct((2, OWN, LANES), F32),
        ),
        in_specs=[vmem] * 2,
        out_specs=(vmem, vmem),
        scratch_shapes=[
            pltpu.VMEM((FIELDS * 16, 384), BF16),
            pltpu.VMEM((FIELDS, BLOCKS, LANES), F32),
            pltpu.VMEM((FIELDS, OWN, LANES), F32),
            pltpu.SemaphoreType.DMA,
            pltpu.SemaphoreType.DMA,
        ],
        compiler_params=remote_params(1 + step),
        name="owner_gather",
    )(table, asked)


def scatter_kernel(
    step, moment_ref, shift_ref, asked_ref, out_ref, loss_ref,
    arrived, high, rest, own_sem, send_sem, recv_sems,
):
    greet()
    me = my_index()
    groups = OWN // BLOCKS
    mine = me // BLOCKS
    all_entered()

    def push(k, _):
        send(moment_ref, arrived, lax.rem(me + k, OWN), send_sem, recv_sems.at[mine])
        return 0

    lax.fori_loop(1, OWN, push, 0, unroll=2)
    own = pltpu.make_async_copy(moment_ref.at[:, me, :], arrived.at[:, me, :], own_sem)
    own.start()
    own.wait()
    low_iota = lax.broadcasted_iota(I32, (128, 128), 0)
    high_iota = lax.broadcasted_iota(I32, (16, 128), 0)

    def landed(group, count):
        blocks = pl.ds(group * BLOCKS, count)
        pltpu.make_async_remote_copy(
            src_ref=moment_ref.at[:, blocks, :],
            dst_ref=arrived.at[:, blocks, :],
            send_sem=send_sem,
            recv_sem=recv_sems.at[group],
            device_id=mesh_place(me),
            device_id_type=pl.DeviceIdType.MESH,
        ).wait_recv()

    def body(k, carry):
        acc, loss = carry
        group = lax.rem(mine + groups - k, groups)

        @pl.when(k == 0)
        def _():
            landed(group, BLOCKS - 1)

        @pl.when(k != 0)
        def _():
            landed(group, BLOCKS)

        first = pl.multiple_of(group * BLOCKS, BLOCKS)
        at = pl.ds(first, BLOCKS)
        local_u, local_v = shift_ref[0, at, :], shift_ref[1, at, :]
        m0, mx, my = arrived[0, at, :], arrived[1, at, :], arrived[2, at, :]
        sx = mx - local_u * m0
        sy = my - local_v * m0
        sums = [
            sx,
            sy,
            arrived[3, at, :] - local_u * (mx + sx),
            arrived[4, at, :] - local_u * my - local_v * sx,
            arrived[5, at, :] - local_v * (my + sy),
            m0,
            arrived[6, at, :],
            arrived[7, at, :],
            arrived[8, at, :],
        ]
        for f in range(FIELDS):
            top = sums[f].astype(BF16).astype(F32)
            high[f] = top
            rest[f] = sums[f] - top
        for pair in range(BLOCKS // 2):
            lefts, rights = [], []
            for half in range(2):
                d = 2 * pair + half
                want = asked_ref[step, pl.ds(first + d, 1), :]
                rights.append(jnp.where(low_iota == (want & 127), 1.0, 0.0).astype(BF16))
                here = high_iota == lax.shift_right_logical(want, 7)
                rows = [
                    jnp.where(here, ref[f, d : d + 1, :], 0.0).astype(BF16)
                    for ref in (high, rest)
                    for f in range(FIELDS)
                ]
                lefts.append(jnp.concatenate(rows, 0))
            acc = acc + lax.dot_general(
                jnp.concatenate(lefts, 1),
                jnp.concatenate(rights, 1),
                (((1,), (1,)), ((), ())),
                preferred_element_type=F32,
            )
        return acc, loss + arrived[FIELDS, at, :]

    acc, loss = lax.fori_loop(
        0,
        groups,
        body,
        (jnp.zeros((2 * FIELDS * 16, 128), F32), jnp.zeros((BLOCKS, LANES), F32)),
    )
    out_ref[...] = acc[: FIELDS * 16] + acc[FIELDS * 16 :]
    loss_ref[...] = jnp.sum(loss, axis=0, keepdims=True)
    all_but_one(moment_ref, arrived, send_sem, own_sem).wait_send()


def owner_scatter(step, moments, shifts, asked):
    vmem = pl.BlockSpec(memory_space=pltpu.VMEM)
    return pl.pallas_call(
        functools.partial(scatter_kernel, step),
        out_shape=(
            jax.ShapeDtypeStruct((FIELDS * 16, 128), F32),
            jax.ShapeDtypeStruct((1, LANES), F32),
        ),
        in_specs=[vmem] * 3,
        out_specs=(vmem, vmem),
        scratch_shapes=[
            pltpu.VMEM((FIELDS + 1, OWN, LANES), F32),
            pltpu.VMEM((FIELDS, BLOCKS, LANES), F32),
            pltpu.VMEM((FIELDS, BLOCKS, LANES), F32),
            pltpu.SemaphoreType.DMA,
            pltpu.SemaphoreType.DMA,
            pltpu.SemaphoreType.DMA((OWN // BLOCKS,)),
        ],
        compiler_params=remote_params(1 + STEPS + step),
        name="owner_scatter",
    )(moments, shifts, asked)


PACK = 8


def render_constants():
    axis = np.arange(SIDE, dtype=np.float32) - 7.5
    x = np.tile(axis, SIDE)
    y = np.repeat(axis, SIDE)
    one = np.ones_like(x)
    zero = np.zeros_like(x)
    block = np.zeros((8, 512), np.float32)
    block[0] = np.concatenate([x, zero])
    block[1] = np.concatenate([y, zero])
    block[2] = np.concatenate([zero, y])
    block[3] = np.concatenate([one, zero])
    block[4] = np.concatenate([zero, one])
    lines = np.concatenate([block, block, block, np.zeros_like(block)], 0)
    mono = np.zeros((2 * PIX, 128), np.float32)
    for k, column in enumerate((one, x, y, x * x, x * y, y * y)):
        mono[:, k * PACK : (k + 1) * PACK] = np.tile(column, 2)[:, None]
    fold = np.zeros((256, 128), np.float32)
    for ch in range(3):
        for half in range(2):
            at = half * 128 + ch * TILES_DEV
            fold[at : at + TILES_DEV, (6 + ch) * PACK : (7 + ch) * PACK] = 1.0
    return jnp.asarray(lines, BF16), jnp.asarray(mono, BF16), jnp.asarray(fold, BF16)


BATCH = 2
COL_OPACITY = 29


def split2(values):
    high = values.astype(BF16)
    return high, (values - high.astype(F32)).astype(BF16)


def render_kernel(
    slot_ref, fields_ref, target_ref, lines_ref, mono_ref, fold_ref,
    picture_ref, moment_ref,
    table, rows, alphas, weights, out_ref, resid, back,
):
    def build(o, _):
        first = fields_ref[0:8, pl.ds(o, 1), :].reshape(8, LANES)
        last = jnp.broadcast_to(fields_ref[8, pl.ds(o, 1), :], (8, LANES))
        stack = jnp.concatenate([*split3(first), first, last], 0)
        table[pl.ds(pl.multiple_of(o * 128, 128), 128), 0:40] = stack.T
        return 0

    lax.fori_loop(0, OWN, build, 0, unroll=4)

    sublane = lax.broadcasted_iota(I32, (8, LANES), 0)

    def fetch(slab, i):
        source = jnp.minimum(slab, SLABS - 1) * 128 + i * TILES_DEV
        for half in range(0, TILES_DEV, 8):
            got = None
            for t in range(8):
                row = table[pl.ds(slot_ref[source + half + t], 1), :]
                row = jnp.broadcast_to(row, (8, LANES))
                got = row if t == 0 else jnp.where(sublane == t, row, got)
            at = pl.multiple_of(slab * 128, 128) + i * TILES_DEV + half
            rows[pl.ds(at, 8), :] = got

    def forward(slab, state):
        through, red, green, blue = state
        for i in range(8):
            at = pl.ds(pl.multiple_of(slab * 128, 128) + i * 16, 16)
            both = jnp.dot(
                rows[at, 0:32].astype(BF16), lines_ref[...], preferred_element_type=F32
            )
            first = both[:, 0:256]
            second = both[:, 256:512]
            cols = rows[at, COL_OPACITY : COL_OPACITY + 4]
            alpha = jnp.exp2(cols[:, 0:1] - first * first - second * second)
            weight = through * alpha
            through = through - weight
            red = red + weight * cols[:, 1:2]
            green = green + weight * cols[:, 2:3]
            blue = blue + weight * cols[:, 3:4]
            alphas[at, :] = alpha
            weights[at, :] = weight
            back[pl.ds(pl.multiple_of(slab * 256, 256) + i * 32, 32), :] = jnp.zeros(
                (32, LANES), F32
            )
            fetch(slab + 1, i)
        return through, red, green, blue

    for i in range(8):
        fetch(0, i)
    blank = jnp.zeros((TILES_DEV, PIX), F32)
    _, red, green, blue = lax.fori_loop(
        0,
        SLABS,
        forward,
        (jnp.ones((TILES_DEV, PIX), F32), blank, blank, blank),
        unroll=4,
    )
    residuals = []
    total = jnp.zeros((), F32)
    for ch, colour in enumerate((red, green, blue)):
        picture_ref[ch] = colour
        residual = colour - target_ref[ch]
        residuals.append(residual)
        total = total + jnp.sum(residual * residual)
    moment_ref[FIELDS] = jnp.full((OWN, LANES), 0.5 * total, F32)
    res_red, res_green, res_blue = residuals

    padded = jnp.concatenate([*residuals, jnp.zeros((80, PIX), F32)], 0)
    turned = padded.T
    top = turned.astype(BF16)
    resid[:, 0:128] = top
    resid[:, 128:256] = (turned - top.astype(F32)).astype(BF16)

    lane = lax.broadcasted_iota(I32, (128, LANES), 1)
    row = lax.broadcasted_iota(I32, (128, LANES), 0)
    own_tile = (lane & 15) == (row & 15)

    def scatter(slab, i, source, base):
        for t in range(TILES_DEV):
            q = i * TILES_DEV + t
            back[pl.ds(slot_ref[slab * 128 + q], 1), :] = source[base + q : base + q + 1, :]

    own_rows = jnp.concatenate([own_tile] * BATCH, 0)

    def backward(turn, behind, target, previous, source):
        first = pl.multiple_of(turn * (BATCH * 128), BATCH * 128)
        every = pl.ds(first, BATCH * 128)
        weight_top, weight_rest = split2(weights[every, :])
        both = jnp.dot(weight_top, resid[...], preferred_element_type=F32)
        shade = both[:, :128] + both[:, 128:]
        shade = shade + jnp.dot(weight_rest, resid[:, 0:128], preferred_element_type=F32)
        shade = jnp.concatenate(split2(jnp.where(own_rows, shade, 0.0)), 1)
        pieces = [None] * (8 * BATCH)
        for i in range(8 * BATCH - 1, -1, -1):
            at = pl.ds(first + i * 16, 16)
            cols = rows[at, COL_OPACITY : COL_OPACITY + 4]
            gain = (
                res_red * cols[:, 1:2] + res_green * cols[:, 2:3] + res_blue * cols[:, 3:4]
            ) - behind
            pieces[i] = weights[at, :] * gain
            behind = behind + alphas[at, :] * gain
            if source is not None:
                scatter(previous * BATCH + i // 8, i % 8, source, i // 8 * 128)
        slope = jnp.concatenate(split2(jnp.concatenate(pieces, 0)), 1)
        target[...] = jnp.dot(slope, mono_ref[...], preferred_element_type=F32) + jnp.dot(
            shade, fold_ref[...], preferred_element_type=F32
        )
        return behind

    batches = SLABS // BATCH
    outs = [out_ref.at[k] for k in range(2)]
    behind = backward(batches - 1, blank, outs[1], None, None)

    def backward_two(k, behind):
        turn = batches - 2 - 2 * k
        behind = backward(turn, behind, outs[0], turn + 1, outs[1])
        return backward(turn - 1, behind, outs[1], turn, outs[0])

    behind = lax.fori_loop(0, batches // 2 - 1, backward_two, behind)
    backward(0, behind, outs[0], 1, outs[1])
    for i in range(8 * BATCH):
        scatter(i // 8, i % 8, outs[0], i // 8 * 128)

    turn = lax.broadcasted_iota(I32, (128, LANES), 1) & (PACK - 1)
    for g in range(OWN // PACK):
        merged = back[g * 1024 : g * 1024 + 128, :]
        for k in range(1, PACK):
            at = g * 1024 + k * 128
            merged = jnp.where(turn == k, back[at : at + 128, :], merged)
        merged = merged.T
        for f in range(FIELDS):
            moment_ref[f, g * PACK : (g + 1) * PACK, :] = merged[f * PACK : (f + 1) * PACK]


def render(slots, fields, target):
    constants = render_constants()
    vmem = pl.BlockSpec(memory_space=pltpu.VMEM)
    entries = SLABS * 128
    return pl.pallas_call(
        render_kernel,
        out_shape=(
            jax.ShapeDtypeStruct((3, TILES_DEV, PIX), F32),
            jax.ShapeDtypeStruct((FIELDS + 1, OWN, LANES), F32),
        ),
        in_specs=[pl.BlockSpec(memory_space=pltpu.SMEM)] + [vmem] * 5,
        out_specs=(vmem, vmem),
        scratch_shapes=[
            pltpu.VMEM((OWN * LANES, LANES), F32),
            pltpu.VMEM((entries + 256, LANES), F32),
            pltpu.VMEM((entries, PIX), F32),
            pltpu.VMEM((entries, PIX), F32),
            pltpu.VMEM((2, BATCH * 128, LANES), F32),
            pltpu.VMEM((PIX, 256), BF16),
            pltpu.VMEM((OWN * LANES, LANES), F32),
        ],
        compiler_params=params_of(56),
        name="render",
    )(slots, fields, target, *constants)


def adam_update(params, moment_one, second, gradient, step_index):
    step_count = adam_start + step_index + 1
    moment_one = beta_one * moment_one + (1.0 - beta_one) * gradient
    second = beta_two * second + (1.0 - beta_two) * gradient * gradient
    scaled_first = moment_one / (1.0 - beta_one**step_count)
    scaled_second = second / (1.0 - beta_two**step_count)
    params = params - learn_rate * scaled_first / (jnp.sqrt(scaled_second) + adam_eps)
    return (params, moment_one, second)


def per_device(gauss_params, first_moment, second_moment, splat_lists, tile_ids, targets, camera):
    local_count = gauss_params.shape[1]
    params, moment_one, moment_two = (gauss_params, first_moment, second_moment)
    ids = jnp.swapaxes(splat_lists, 1, 2).reshape(STEPS, SLABS, LANES)
    lane_tiles = jnp.tile(tile_ids, (1, LANES // TILES_DEV))
    slots, asked = routing(ids, lane_tiles[:, None, :])
    slots = slots.reshape(STEPS, SLABS * LANES)
    pictures = []
    losses = []
    for step_index in range(STEPS):
        projected, pullback, inverses = jax.vjp(
            lambda values: project(values, camera[step_index]), params, has_aux=True
        )
        table = factor_rows(projected, inverses).reshape(FIELDS, 16, 128)
        fields, shifts = owner_gather(step_index, table, asked)
        target = jnp.swapaxes(targets[step_index], 0, 1)
        picture, moments = render(slots[step_index], fields, target)
        sums, loss = owner_scatter(step_index, moments, shifts, asked)
        sums = sums.reshape(FIELDS, local_count)
        losses.append(loss[0, 0])
        conic_a, conic_b, conic_c = projected[2], projected[3], projected[4]
        cotangent = jnp.concatenate(
            [
                jnp.stack(
                    [
                        conic_a * sums[0] + conic_b * sums[1],
                        conic_b * sums[0] + conic_c * sums[1],
                        -0.5 * sums[2],
                        -sums[3],
                        -0.5 * sums[4],
                    ]
                ),
                sums[5:9],
            ],
            0,
        )
        gradient = pullback(cotangent)[0]
        params, moment_one, moment_two = adam_update(
            params, moment_one, moment_two, gradient, step_index
        )
        pictures.append(jnp.swapaxes(picture, 0, 1))
    loss_values = jnp.stack(losses) / (3.0 * PIX * TILES_DEV * OWN)
    return (params, moment_one, moment_two, jnp.stack(pictures), loss_values)


def solution(mesh):
    both = ("gx", "gy")
    in_specs = (
        P(None, both),
        P(None, both),
        P(None, both),
        P(None, both, None),
        P(None, both),
        P(None, both, None, None),
        P(),
    )
    out_specs = (
        P(None, both),
        P(None, both),
        P(None, both),
        P(None, both, None, None),
        P(),
    )
    return jax.shard_map(
        per_device, mesh=mesh, in_specs=in_specs, out_specs=out_specs, check_vma=False
    )
```

```python
import functools
import math

import jax
import jax.numpy as jnp
import numpy as np
from jax import lax
from jax.experimental import pallas as pl
from jax.experimental.pallas import tpu as pltpu
from jax.sharding import PartitionSpec as P

SIDE = 16
PIX = 256
NCOEF = 16
STEPS = 2
IMG_TX = 64
IMG_TY = 32
OWN = 128
LANES = 128
TILES_DEV = 16
LIST = 512
SLABS = LIST * TILES_DEV // 128
FIELDS = 9
F32 = jnp.float32
BF16 = jnp.bfloat16
I32 = jnp.int32

beta_one = 0.9
beta_two = 0.999
adam_eps = 1e-08
learn_rate = 0.01
adam_start = 1000
band_zero = 0.28209479177387814
band_one = 0.4886025119029199
band_two = (
    1.0925484305920792,
    -1.0925484305920792,
    0.31539156525252005,
    -1.0925484305920792,
    0.5462742152960396,
)
band_three = (
    -0.5900435899266435,
    2.890611442640554,
    -0.4570457994644658,
    0.3731763325901154,
    -0.4570457994644658,
    1.445305721320277,
    -0.5900435899266435,
)
half_log2e = math.sqrt(0.5 * math.log2(math.e))


def params_of(megabytes):
    return pltpu.CompilerParams(vmem_limit_bytes=megabytes << 20)


def harmonics(ray_x, ray_y, ray_z):
    sq_x = ray_x * ray_x
    sq_y = ray_y * ray_y
    sq_z = ray_z * ray_z
    return jnp.stack(
        [
            band_zero * jnp.ones_like(ray_x),
            -band_one * ray_y,
            band_one * ray_z,
            -band_one * ray_x,
            band_two[0] * ray_x * ray_y,
            band_two[1] * ray_y * ray_z,
            band_two[2] * (2.0 * sq_z - sq_x - sq_y),
            band_two[3] * ray_x * ray_z,
            band_two[4] * (sq_x - sq_y),
            band_three[0] * ray_y * (3.0 * sq_x - sq_y),
            band_three[1] * ray_x * ray_y * ray_z,
            band_three[2] * ray_y * (4.0 * sq_z - sq_x - sq_y),
            band_three[3] * ray_z * (2.0 * sq_z - 3.0 * sq_x - 3.0 * sq_y),
            band_three[4] * ray_x * (4.0 * sq_z - sq_x - sq_y),
            band_three[5] * ray_z * (sq_x - sq_y),
            band_three[6] * ray_x * (sq_x - 3.0 * sq_y),
        ]
    )


def project(gauss_rows, camera_row):
    image_width = 1.0 * SIDE * IMG_TX
    image_height = 1.0 * SIDE * IMG_TY
    depth_z = gauss_rows[2]
    screen_u = (gauss_rows[0] - camera_row[0]) / depth_z
    screen_v = (gauss_rows[1] - camera_row[1]) / depth_z
    inv_one = depth_z * depth_z * jnp.exp(-2.0 * gauss_rows[3])
    inv_two = depth_z * depth_z * jnp.exp(-2.0 * gauss_rows[4])
    cosine = jnp.cos(gauss_rows[5])
    sine_angle = jnp.sin(gauss_rows[5])
    conic_a = cosine * cosine * inv_one + sine_angle * sine_angle * inv_two
    conic_b = cosine * sine_angle * (inv_one - inv_two)
    conic_c = sine_angle * sine_angle * inv_one + cosine * cosine * inv_two
    log_opacity = math.log(0.99) - jax.nn.softplus(-gauss_rows[6])
    ray_x = (screen_u - 0.5 * image_width) / image_width
    ray_y = (screen_v - 0.5 * image_height) / image_width
    factor = lax.rsqrt(ray_x * ray_x + ray_y * ray_y + 1.0)
    harmonic_basis = harmonics(ray_x * factor, ray_y * factor, factor)
    coeffs = gauss_rows[7:].reshape(3, NCOEF, gauss_rows.shape[1])
    colour = 0.5 + jnp.sum(coeffs * harmonic_basis[None], axis=1)
    geometry = jnp.stack([screen_u, screen_v, conic_a, conic_b, conic_c, log_opacity])
    return jnp.concatenate([geometry, colour], 0), (inv_one, inv_two)


def factor_rows(projected, inverses):
    conic_a, conic_b, conic_c = projected[2], projected[3], projected[4]
    inv_one, inv_two = inverses
    has_a = conic_a > 0.0
    safe_a = jnp.where(has_a, conic_a, 1.0)
    root = jnp.sqrt(safe_a)
    alpha = jnp.where(has_a, half_log2e * root, 0.0)
    beta = jnp.where(has_a, half_log2e * conic_b / root, 0.0)
    gamma = half_log2e * jnp.where(
        has_a, jnp.sqrt(inv_one * (inv_two / safe_a)), jnp.sqrt(conic_c)
    )
    log2_opacity = jnp.maximum(projected[5] * math.log2(math.e), -1.0e4)
    return jnp.concatenate(
        [projected[0:2], jnp.stack([alpha, beta, gamma, log2_opacity]), projected[6:9]], 0
    )


def split3(values):
    hi = values.astype(BF16).astype(F32)
    rest = values - hi
    mid = rest.astype(BF16).astype(F32)
    return hi, mid, rest - mid


def my_index():
    return lax.axis_index("gx") * lax.axis_size("gy") + lax.axis_index("gy")


def mesh_place(device):
    inner = lax.axis_size("gy")
    return (device // inner, lax.rem(device, inner))


CHIPS = OWN // 2


def my_chip_core():
    me = my_index()
    return me // 2, lax.rem(me, 2)


def greet():
    barrier = pltpu.get_barrier_semaphore()
    chip, core = my_chip_core()

    def tell(device):
        pl.semaphore_signal(
            barrier,
            inc=1,
            device_id=mesh_place(device),
            device_id_type=pl.DeviceIdType.MESH,
        )

    tell(2 * chip + 1 - core)

    def one(k, _):
        tell(2 * lax.rem(chip + k, CHIPS) + core)
        return 0

    lax.fori_loop(1, CHIPS, one, 0, unroll=3)


def all_entered():
    pl.semaphore_wait(pltpu.get_barrier_semaphore(), CHIPS)


def to_sibling(source, mixed, send_sem, recv_sem):
    chip, core = my_chip_core()
    return pltpu.make_async_remote_copy(
        src_ref=source,
        dst_ref=mixed.at[:, core, :, :],
        send_sem=send_sem,
        recv_sem=recv_sem,
        device_id=mesh_place(2 * chip + 1 - core),
        device_id_type=pl.DeviceIdType.MESH,
    )


def to_chip(peer, mixed, target, send_sem, recv_sem):
    chip, core = my_chip_core()
    pltpu.make_async_remote_copy(
        src_ref=mixed.at[:, :, peer, :],
        dst_ref=target.at[:, :, chip, :],
        send_sem=send_sem,
        recv_sem=recv_sem,
        device_id=mesh_place(2 * peer + core),
        device_id_type=pl.DeviceIdType.MESH,
    ).start()


def bytes_of(first, count, mixed, target, send_sem, recv_sem):
    chips = pl.ds(first, count)
    return pltpu.make_async_remote_copy(
        src_ref=mixed.at[:, :, chips, :],
        dst_ref=target.at[:, :, chips, :],
        send_sem=send_sem,
        recv_sem=recv_sem,
        device_id=mesh_place(my_index()),
        device_id_type=pl.DeviceIdType.MESH,
    )


def keep_own(mixed, target):
    chip, _ = my_chip_core()
    for k in range(mixed.shape[0]):
        for core in range(2):
            target[k, core, pl.ds(chip, 1), :] = mixed[k, core, pl.ds(chip, 1), :]


def remote_params(collective_id, megabytes=32):
    return pltpu.CompilerParams(
        collective_id=collective_id, has_side_effects=True, vmem_limit_bytes=megabytes << 20
    )


GROUP = 4


def routing_kernel(ids_ref, tile_ref, upper_ref, slot_ref, asked_ref, request, mixed, send_sem, recv_sem,
    near_send, near_recv,
):
    greet()
    row_iota = lax.broadcasted_iota(I32, (OWN, LANES), 0)
    own_tile = (lax.broadcasted_iota(I32, (1, LANES), 1) & (TILES_DEV - 1)).astype(F32)
    zero = jnp.zeros((OWN, LANES), F32)
    upper = upper_ref[...]

    def body(k, carry):
        out = []
        for s in range(STEPS):
            counts, acc = carry[s]
            members, cells = [], []
            for c in range(GROUP):
                ids = ids_ref[s, pl.ds(k * GROUP + c, 1), :]
                owner = lax.shift_right_logical(ids, 12) + (lax.shift_right_logical(ids, 11) & 1) * CHIPS
                member = row_iota == owner
                member_bf = jnp.where(member, 1.0, 0.0).astype(BF16)
                ahead = jnp.dot(member_bf, upper, preferred_element_type=F32)
                rank = jnp.sum(
                    jnp.where(member, ahead[:, :LANES] + counts, 0.0), axis=0, keepdims=True
                ).astype(I32)
                counts = counts + ahead[:, LANES:]
                slot_ref[s, pl.ds(k * GROUP + c, 1), :] = owner * LANES + rank
                here = row_iota == rank
                low = (ids & 127).astype(F32)
                high = (lax.shift_right_logical(ids, 7) & 15).astype(F32) * 16.0 + own_tile
                members.append(member_bf)
                cells.append(
                    jnp.concatenate(
                        [
                            jnp.where(here, low, 0.0).astype(BF16),
                            jnp.where(here, high, 0.0).astype(BF16),
                        ],
                        0,
                    )
                )
            acc = acc + lax.dot_general(
                jnp.concatenate(members, 1),
                jnp.concatenate(cells, 1),
                (((1,), (1,)), ((), ())),
                preferred_element_type=F32,
            )
            out.append((counts, acc))
        return tuple(out)

    start = tuple((zero, jnp.zeros((OWN, 2 * LANES), F32)) for _ in range(STEPS))
    done = lax.fori_loop(0, SLABS // GROUP, body, start)
    for s in range(STEPS):
        acc = done[s][1].astype(I32)
        high = acc[:, LANES:]
        want = acc[:, :LANES] + lax.shift_right_logical(high, 4) * 128
        request[s] = want.reshape(2, CHIPS, LANES)
        tile = jnp.take_along_axis(
            jnp.broadcast_to(tile_ref[s], (OWN, LANES)),
            high & 15,
            axis=1,
            mode="promise_in_bounds",
        )
        request[STEPS + s] = tile.reshape(2, CHIPS, LANES)
    all_entered()
    chip, core = my_chip_core()
    near = to_sibling(request.at[:, 1 - core, :, :], mixed, near_send, near_recv)
    near.start()
    for k in range(2 * STEPS):
        mixed[k, core] = request[k, core]
    near.wait()

    def push(k, _):
        to_chip(lax.rem(chip + k, CHIPS), mixed, asked_ref, send_sem, recv_sem)
        return 0

    lax.fori_loop(1, CHIPS, push, 0, unroll=3)
    keep_own(mixed, asked_ref)
    rest = bytes_of(0, CHIPS - 1, mixed, asked_ref, send_sem, recv_sem)
    rest.wait_send()
    rest.wait_recv()


def routing(ids, lane_tiles):
    strict = np.triu(np.ones((128, 128), np.float32), 1)
    upper = jnp.asarray(np.concatenate([strict, np.ones((128, 128), np.float32)], 1), BF16)
    vmem = pl.BlockSpec(memory_space=pltpu.VMEM)
    return pl.pallas_call(
        routing_kernel,
        out_shape=(
            jax.ShapeDtypeStruct((STEPS, SLABS, LANES), I32),
            jax.ShapeDtypeStruct((2 * STEPS, 2, CHIPS, LANES), I32),
        ),
        in_specs=[vmem] * 3,
        out_specs=(vmem, vmem),
        scratch_shapes=[
            pltpu.VMEM((2 * STEPS, 2, CHIPS, LANES), I32),
            pltpu.VMEM((2 * STEPS, 2, CHIPS, LANES), I32),
            pltpu.SemaphoreType.DMA,
            pltpu.SemaphoreType.DMA,
            pltpu.SemaphoreType.DMA,
            pltpu.SemaphoreType.DMA,
        ],
        compiler_params=remote_params(0),
        name="routing",
    )(ids, lane_tiles, upper)


BLOCKS = 8


def gather_kernel(
    step, table_ref, asked_ref, out_ref, shift_ref, parts, got, answer, mixed, send_sem, recv_sem,
    near_send, near_recv,
):
    greet()
    for f in range(FIELDS):
        for p, part in enumerate(split3(table_ref[f])):
            parts[f * 16 : f * 16 + 16, p * 128 : p * 128 + 128] = part.astype(BF16)
    low_iota = lax.broadcasted_iota(I32, (128, 256), 0)
    high_iota = lax.broadcasted_iota(I32, (16, 256), 0)
    chip, core = my_chip_core()
    groups = CHIPS // BLOCKS

    def group_of(k):
        return lax.rem(chip // BLOCKS + k, groups)

    def compute(group, receiver):
        first = pl.multiple_of(receiver * CHIPS + group * BLOCKS, BLOCKS)
        for pair in range(BLOCKS // 2):
            d = first + 2 * pair
            want = jnp.concatenate(
                [asked_ref[step, pl.ds(d, 1), :], asked_ref[step, pl.ds(d + 1, 1), :]], 1
            )
            hot = jnp.where(low_iota == (want & 127), 1.0, 0.0).astype(BF16)
            hot = jnp.concatenate([hot, hot, hot], 0)
            here = high_iota == lax.shift_right_logical(want, 7)
            picked = jnp.dot(parts[...], hot, preferred_element_type=F32)
            for f in range(FIELDS):
                row = jnp.sum(
                    jnp.where(here, picked[f * 16 : f * 16 + 16], 0.0), axis=0, keepdims=True
                )
                got[f, 2 * pair : 2 * pair + 1, :] = row[:, :128]
                got[f, 2 * pair + 1 : 2 * pair + 2, :] = row[:, 128:]
        at = pl.ds(first, BLOCKS)
        tile = asked_ref[STEPS + step, at, :]
        centre_x = ((tile & (IMG_TX - 1)) * SIDE + SIDE // 2).astype(F32)
        centre_y = (lax.shift_right_logical(tile, 6) * SIDE + SIDE // 2).astype(F32)
        local_u = got[0] - centre_x
        local_v = got[1] - centre_y
        shift_ref[0, at, :] = local_u
        shift_ref[1, at, :] = local_v
        alpha, beta, gamma = got[2], got[3], got[4]
        chips = pl.ds(pl.multiple_of(group * BLOCKS, BLOCKS), BLOCKS)
        values = [
            alpha,
            beta,
            gamma,
            -(alpha * local_u + beta * local_v),
            -gamma * local_v,
            *[got[f] for f in range(5, FIELDS)],
        ]
        return chips, values

    def others(k, _):
        chips, values = compute(group_of(k), 1 - core)
        for f in range(FIELDS):
            answer[f, chips, :] = values[f]
        return 0

    lax.fori_loop(0, groups, others, 0)
    all_entered()
    near = to_sibling(answer, mixed, near_send, near_recv)
    near.start()

    def ours(k):
        chips, values = compute(group_of(k), core)
        for f in range(FIELDS):
            mixed[f, core, chips, :] = values[f]

    def push(group):
        for k in range(BLOCKS):
            peer = group * BLOCKS + lax.rem(chip + k, BLOCKS)
            to_chip(peer, mixed, out_ref, send_sem, recv_sem)

    def early(k, _):
        ours(k)
        return 0

    lax.fori_loop(0, groups // 2, early, 0)
    near.wait()

    def late(k, _):
        push(group_of(k - groups // 2 + 1))
        ours(k)
        return 0

    lax.fori_loop(groups // 2, groups, late, 0)

    def last(k, _):
        push(group_of(k))
        return 0

    lax.fori_loop(groups // 2 + 1, groups, last, 0)

    def inside(k, _):
        peer = chip // BLOCKS * BLOCKS + lax.rem(chip + k, BLOCKS)
        to_chip(peer, mixed, out_ref, send_sem, recv_sem)
        return 0

    lax.fori_loop(1, BLOCKS, inside, 0)
    keep_own(mixed, out_ref)
    rest = bytes_of(0, CHIPS - 1, mixed, out_ref, send_sem, recv_sem)
    rest.wait_send()
    rest.wait_recv()


def owner_gather(step, table, asked):
    vmem = pl.BlockSpec(memory_space=pltpu.VMEM)
    return pl.pallas_call(
        functools.partial(gather_kernel, step),
        out_shape=(
            jax.ShapeDtypeStruct((FIELDS, 2, CHIPS, LANES), F32),
            jax.ShapeDtypeStruct((2, OWN, LANES), F32),
        ),
        in_specs=[vmem] * 2,
        out_specs=(vmem, vmem),
        scratch_shapes=[
            pltpu.VMEM((FIELDS * 16, 384), BF16),
            pltpu.VMEM((FIELDS, BLOCKS, LANES), F32),
            pltpu.VMEM((FIELDS, CHIPS, LANES), F32),
            pltpu.VMEM((FIELDS, 2, CHIPS, LANES), F32),
            pltpu.SemaphoreType.DMA,
            pltpu.SemaphoreType.DMA,
            pltpu.SemaphoreType.DMA,
            pltpu.SemaphoreType.DMA,
        ],
        compiler_params=remote_params(1 + step),
        name="owner_gather",
    )(table, asked)


def scatter_kernel(
    step, moment_ref, shift_ref, asked_ref, out_ref, loss_ref,
    arrived, high, rest, mixed, near_send, near_recv, send_sem, recv_sems,
):
    greet()
    chip, core = my_chip_core()
    groups = CHIPS // BLOCKS
    mine = chip // BLOCKS
    all_entered()
    near = to_sibling(moment_ref.at[:, 1 - core, :, :], mixed, near_send, near_recv)
    near.start()
    for k in range(FIELDS + 1):
        mixed[k, core] = moment_ref[k, core]
    near.wait()

    def push(k, _):
        to_chip(lax.rem(chip + k, CHIPS), mixed, arrived, send_sem, recv_sems.at[mine])
        return 0

    lax.fori_loop(1, CHIPS, push, 0, unroll=3)
    keep_own(mixed, arrived)
    low_iota = lax.broadcasted_iota(I32, (128, 128), 0)
    high_iota = lax.broadcasted_iota(I32, (16, 128), 0)

    def landed(group, count):
        first = group * BLOCKS
        bytes_of(first, count, mixed, arrived, send_sem, recv_sems.at[group]).wait_recv()

    def body(k, carry):
        acc, loss = carry
        group = lax.rem(mine + groups - k, groups)

        @pl.when(k == 0)
        def _():
            landed(group, BLOCKS - 1)

        @pl.when(k != 0)
        def _():
            landed(group, BLOCKS)

        for sender in range(2):
            chips = pl.ds(pl.multiple_of(group * BLOCKS, BLOCKS), BLOCKS)
            first = pl.multiple_of(sender * CHIPS + group * BLOCKS, BLOCKS)
            at = pl.ds(first, BLOCKS)
            local_u, local_v = shift_ref[0, at, :], shift_ref[1, at, :]
            m0, mx, my = arrived[0, sender, chips, :], arrived[1, sender, chips, :], arrived[2, sender, chips, :]
            sx = mx - local_u * m0
            sy = my - local_v * m0
            sums = [
                sx,
                sy,
                arrived[3, sender, chips, :] - local_u * (mx + sx),
                arrived[4, sender, chips, :] - local_u * my - local_v * sx,
                arrived[5, sender, chips, :] - local_v * (my + sy),
                m0,
                arrived[6, sender, chips, :],
                arrived[7, sender, chips, :],
                arrived[8, sender, chips, :],
            ]
            for f in range(FIELDS):
                top = sums[f].astype(BF16).astype(F32)
                high[f] = top
                rest[f] = sums[f] - top
            for pair in range(BLOCKS // 2):
                lefts, rights = [], []
                for half in range(2):
                    d = 2 * pair + half
                    want = asked_ref[step, pl.ds(first + d, 1), :]
                    rights.append(jnp.where(low_iota == (want & 127), 1.0, 0.0).astype(BF16))
                    here = high_iota == lax.shift_right_logical(want, 7)
                    rows = [
                        jnp.where(here, ref[f, d : d + 1, :], 0.0).astype(BF16)
                        for ref in (high, rest)
                        for f in range(FIELDS)
                    ]
                    lefts.append(jnp.concatenate(rows, 0))
                acc = acc + lax.dot_general(
                    jnp.concatenate(lefts, 1),
                    jnp.concatenate(rights, 1),
                    (((1,), (1,)), ((), ())),
                    preferred_element_type=F32,
                )
            loss = loss + arrived[FIELDS, sender, chips, :]
        return acc, loss

    acc, loss = lax.fori_loop(
        0,
        groups,
        body,
        (jnp.zeros((2 * FIELDS * 16, 128), F32), jnp.zeros((BLOCKS, LANES), F32)),
    )
    out_ref[...] = acc[: FIELDS * 16] + acc[FIELDS * 16 :]
    loss_ref[...] = jnp.sum(loss, axis=0, keepdims=True)
    bytes_of(0, CHIPS - 1, mixed, arrived, send_sem, near_recv).wait_send()


def owner_scatter(step, moments, shifts, asked):
    vmem = pl.BlockSpec(memory_space=pltpu.VMEM)
    return pl.pallas_call(
        functools.partial(scatter_kernel, step),
        out_shape=(
            jax.ShapeDtypeStruct((FIELDS * 16, 128), F32),
            jax.ShapeDtypeStruct((1, LANES), F32),
        ),
        in_specs=[vmem] * 3,
        out_specs=(vmem, vmem),
        scratch_shapes=[
            pltpu.VMEM((FIELDS + 1, 2, CHIPS, LANES), F32),
            pltpu.VMEM((FIELDS, BLOCKS, LANES), F32),
            pltpu.VMEM((FIELDS, BLOCKS, LANES), F32),
            pltpu.VMEM((FIELDS + 1, 2, CHIPS, LANES), F32),
            pltpu.SemaphoreType.DMA,
            pltpu.SemaphoreType.DMA,
            pltpu.SemaphoreType.DMA,
            pltpu.SemaphoreType.DMA((CHIPS // BLOCKS,)),
        ],
        compiler_params=remote_params(1 + STEPS + step),
        name="owner_scatter",
    )(moments, shifts, asked)


PACK = 8


def render_constants():
    axis = np.arange(SIDE, dtype=np.float32) - 7.5
    x = np.tile(axis, SIDE)
    y = np.repeat(axis, SIDE)
    one = np.ones_like(x)
    zero = np.zeros_like(x)
    block = np.zeros((8, 512), np.float32)
    block[0] = np.concatenate([x, zero])
    block[1] = np.concatenate([y, zero])
    block[2] = np.concatenate([zero, y])
    block[3] = np.concatenate([one, zero])
    block[4] = np.concatenate([zero, one])
    lines = np.concatenate([block, block, block, np.zeros_like(block)], 0)
    mono = np.zeros((2 * PIX, 128), np.float32)
    for k, column in enumerate((one, x, y, x * x, x * y, y * y)):
        mono[:, k * PACK : (k + 1) * PACK] = np.tile(column, 2)[:, None]
    fold = np.zeros((256, 128), np.float32)
    for ch in range(3):
        for half in range(2):
            at = half * 128 + ch * TILES_DEV
            fold[at : at + TILES_DEV, (6 + ch) * PACK : (7 + ch) * PACK] = 1.0
    return jnp.asarray(lines, BF16), jnp.asarray(mono, BF16), jnp.asarray(fold, BF16)


BATCH = 2
COL_OPACITY = 29


def split2(values):
    high = values.astype(BF16)
    return high, (values - high.astype(F32)).astype(BF16)


def render_kernel(
    slot_ref, fields_ref, target_ref, lines_ref, mono_ref, fold_ref,
    picture_ref, moment_ref,
    table, rows, alphas, weights, out_ref, resid, back,
):
    def build(o, _):
        first = fields_ref[0:8, pl.ds(o, 1), :].reshape(8, LANES)
        last = jnp.broadcast_to(fields_ref[8, pl.ds(o, 1), :], (8, LANES))
        stack = jnp.concatenate([*split3(first), first, last], 0)
        table[pl.ds(pl.multiple_of(o * 128, 128), 128), 0:40] = stack.T
        return 0

    lax.fori_loop(0, OWN, build, 0, unroll=4)

    sublane = lax.broadcasted_iota(I32, (8, LANES), 0)

    def fetch(slab, i):
        source = jnp.minimum(slab, SLABS - 1) * 128 + i * TILES_DEV
        for half in range(0, TILES_DEV, 8):
            got = None
            for t in range(8):
                row = table[pl.ds(slot_ref[source + half + t], 1), :]
                row = jnp.broadcast_to(row, (8, LANES))
                got = row if t == 0 else jnp.where(sublane == t, row, got)
            at = pl.multiple_of(slab * 128, 128) + i * TILES_DEV + half
            rows[pl.ds(at, 8), :] = got

    def forward(slab, state):
        through, red, green, blue = state
        for i in range(8):
            at = pl.ds(pl.multiple_of(slab * 128, 128) + i * 16, 16)
            both = jnp.dot(
                rows[at, 0:32].astype(BF16), lines_ref[...], preferred_element_type=F32
            )
            first = both[:, 0:256]
            second = both[:, 256:512]
            cols = rows[at, COL_OPACITY : COL_OPACITY + 4]
            alpha = jnp.exp2(cols[:, 0:1] - first * first - second * second)
            weight = through * alpha
            through = through - weight
            red = red + weight * cols[:, 1:2]
            green = green + weight * cols[:, 2:3]
            blue = blue + weight * cols[:, 3:4]
            alphas[at, :] = alpha
            weights[at, :] = weight
            back[pl.ds(pl.multiple_of(slab * 256, 256) + i * 32, 32), :] = jnp.zeros(
                (32, LANES), F32
            )
            fetch(slab + 1, i)
        return through, red, green, blue

    for i in range(8):
        fetch(0, i)
    blank = jnp.zeros((TILES_DEV, PIX), F32)
    _, red, green, blue = lax.fori_loop(
        0,
        SLABS,
        forward,
        (jnp.ones((TILES_DEV, PIX), F32), blank, blank, blank),
        unroll=4,
    )
    residuals = []
    total = jnp.zeros((), F32)
    for ch, colour in enumerate((red, green, blue)):
        picture_ref[ch] = colour
        residual = colour - target_ref[ch]
        residuals.append(residual)
        total = total + jnp.sum(residual * residual)
    moment_ref[FIELDS] = jnp.full((OWN, LANES), 0.5 * total, F32)
    res_red, res_green, res_blue = residuals

    padded = jnp.concatenate([*residuals, jnp.zeros((80, PIX), F32)], 0)
    turned = padded.T
    top = turned.astype(BF16)
    resid[:, 0:128] = top
    resid[:, 128:256] = (turned - top.astype(F32)).astype(BF16)

    lane = lax.broadcasted_iota(I32, (128, LANES), 1)
    row = lax.broadcasted_iota(I32, (128, LANES), 0)
    own_tile = (lane & 15) == (row & 15)

    def scatter(slab, i, source, base):
        for t in range(TILES_DEV):
            q = i * TILES_DEV + t
            back[pl.ds(slot_ref[slab * 128 + q], 1), :] = source[base + q : base + q + 1, :]

    own_rows = jnp.concatenate([own_tile] * BATCH, 0)

    def backward(turn, behind, target, previous, source):
        first = pl.multiple_of(turn * (BATCH * 128), BATCH * 128)
        every = pl.ds(first, BATCH * 128)
        weight_top, weight_rest = split2(weights[every, :])
        both = jnp.dot(weight_top, resid[...], preferred_element_type=F32)
        shade = both[:, :128] + both[:, 128:]
        shade = shade + jnp.dot(weight_rest, resid[:, 0:128], preferred_element_type=F32)
        shade = jnp.concatenate(split2(jnp.where(own_rows, shade, 0.0)), 1)
        pieces = [None] * (8 * BATCH)
        for i in range(8 * BATCH - 1, -1, -1):
            at = pl.ds(first + i * 16, 16)
            cols = rows[at, COL_OPACITY : COL_OPACITY + 4]
            gain = (
                res_red * cols[:, 1:2] + res_green * cols[:, 2:3] + res_blue * cols[:, 3:4]
            ) - behind
            pieces[i] = weights[at, :] * gain
            behind = behind + alphas[at, :] * gain
            if source is not None:
                scatter(previous * BATCH + i // 8, i % 8, source, i // 8 * 128)
        slope = jnp.concatenate(split2(jnp.concatenate(pieces, 0)), 1)
        target[...] = jnp.dot(slope, mono_ref[...], preferred_element_type=F32) + jnp.dot(
            shade, fold_ref[...], preferred_element_type=F32
        )
        return behind

    batches = SLABS // BATCH
    outs = [out_ref.at[k] for k in range(2)]
    behind = backward(batches - 1, blank, outs[1], None, None)

    def backward_two(k, behind):
        turn = batches - 2 - 2 * k
        behind = backward(turn, behind, outs[0], turn + 1, outs[1])
        return backward(turn - 1, behind, outs[1], turn, outs[0])

    behind = lax.fori_loop(0, batches // 2 - 1, backward_two, behind)
    backward(0, behind, outs[0], 1, outs[1])
    for i in range(8 * BATCH):
        scatter(i // 8, i % 8, outs[0], i // 8 * 128)

    turn = lax.broadcasted_iota(I32, (128, LANES), 1) & (PACK - 1)
    for g in range(OWN // PACK):
        merged = back[g * 1024 : g * 1024 + 128, :]
        for k in range(1, PACK):
            at = g * 1024 + k * 128
            merged = jnp.where(turn == k, back[at : at + 128, :], merged)
        merged = merged.T
        for f in range(FIELDS):
            moment_ref[f, g * PACK : (g + 1) * PACK, :] = merged[f * PACK : (f + 1) * PACK]


def render(slots, fields, target):
    constants = render_constants()
    vmem = pl.BlockSpec(memory_space=pltpu.VMEM)
    entries = SLABS * 128
    return pl.pallas_call(
        render_kernel,
        out_shape=(
            jax.ShapeDtypeStruct((3, TILES_DEV, PIX), F32),
            jax.ShapeDtypeStruct((FIELDS + 1, OWN, LANES), F32),
        ),
        in_specs=[pl.BlockSpec(memory_space=pltpu.SMEM)] + [vmem] * 5,
        out_specs=(vmem, vmem),
        scratch_shapes=[
            pltpu.VMEM((OWN * LANES, LANES), F32),
            pltpu.VMEM((entries + 256, LANES), F32),
            pltpu.VMEM((entries, PIX), F32),
            pltpu.VMEM((entries, PIX), F32),
            pltpu.VMEM((2, BATCH * 128, LANES), F32),
            pltpu.VMEM((PIX, 256), BF16),
            pltpu.VMEM((OWN * LANES, LANES), F32),
        ],
        compiler_params=params_of(56),
        name="render",
    )(slots, fields, target, *constants)


def adam_update(params, moment_one, second, gradient, step_index):
    step_count = adam_start + step_index + 1
    moment_one = beta_one * moment_one + (1.0 - beta_one) * gradient
    second = beta_two * second + (1.0 - beta_two) * gradient * gradient
    scaled_first = moment_one / (1.0 - beta_one**step_count)
    scaled_second = second / (1.0 - beta_two**step_count)
    params = params - learn_rate * scaled_first / (jnp.sqrt(scaled_second) + adam_eps)
    return (params, moment_one, second)


def per_device(gauss_params, first_moment, second_moment, splat_lists, tile_ids, targets, camera):
    local_count = gauss_params.shape[1]
    params, moment_one, moment_two = (gauss_params, first_moment, second_moment)
    ids = jnp.swapaxes(splat_lists, 1, 2).reshape(STEPS, SLABS, LANES)
    lane_tiles = jnp.tile(tile_ids, (1, LANES // TILES_DEV))
    slots, asked = routing(ids, lane_tiles[:, None, :])
    slots = slots.reshape(STEPS, SLABS * LANES)
    asked = asked.reshape(2 * STEPS, OWN, LANES)
    pictures = []
    losses = []
    for step_index in range(STEPS):
        projected, pullback, inverses = jax.vjp(
            lambda values: project(values, camera[step_index]), params, has_aux=True
        )
        table = factor_rows(projected, inverses).reshape(FIELDS, 16, 128)
        fields, shifts = owner_gather(step_index, table, asked)
        fields = fields.reshape(FIELDS, OWN, LANES)
        target = jnp.swapaxes(targets[step_index], 0, 1)
        picture, moments = render(slots[step_index], fields, target)
        moments = moments.reshape(FIELDS + 1, 2, CHIPS, LANES)
        sums, loss = owner_scatter(step_index, moments, shifts, asked)
        sums = sums.reshape(FIELDS, local_count)
        losses.append(loss[0, 0])
        conic_a, conic_b, conic_c = projected[2], projected[3], projected[4]
        cotangent = jnp.concatenate(
            [
                jnp.stack(
                    [
                        conic_a * sums[0] + conic_b * sums[1],
                        conic_b * sums[0] + conic_c * sums[1],
                        -0.5 * sums[2],
                        -sums[3],
                        -0.5 * sums[4],
                    ]
                ),
                sums[5:9],
            ],
            0,
        )
        gradient = pullback(cotangent)[0]
        params, moment_one, moment_two = adam_update(
            params, moment_one, moment_two, gradient, step_index
        )
        pictures.append(jnp.swapaxes(picture, 0, 1))
    loss_values = jnp.stack(losses) / (3.0 * PIX * TILES_DEV * OWN)
    return (params, moment_one, moment_two, jnp.stack(pictures), loss_values)


def solution(mesh):
    both = ("gx", "gy")
    in_specs = (
        P(None, both),
        P(None, both),
        P(None, both),
        P(None, both, None),
        P(None, both),
        P(None, both, None, None),
        P(),
    )
    out_specs = (
        P(None, both),
        P(None, both),
        P(None, both),
        P(None, both, None, None),
        P(),
    )
    return jax.shard_map(
        per_device, mesh=mesh, in_specs=in_specs, out_specs=out_specs, check_vma=False
    )
```

```python
import functools
import math

import jax
import jax.numpy as jnp
import numpy as np
from jax import lax
from jax.experimental import pallas as pl
from jax.experimental.pallas import tpu as pltpu
from jax.sharding import PartitionSpec as P

SIDE = 16
PIX = 256
NCOEF = 16
STEPS = 2
IMG_TX = 64
IMG_TY = 32
OWN = 128
LANES = 128
TILES_DEV = 16
LIST = 512
SLABS = LIST * TILES_DEV // 128
FIELDS = 9
F32 = jnp.float32
BF16 = jnp.bfloat16
I32 = jnp.int32

beta_one = 0.9
beta_two = 0.999
adam_eps = 1e-08
learn_rate = 0.01
adam_start = 1000
band_zero = 0.28209479177387814
band_one = 0.4886025119029199
band_two = (
    1.0925484305920792,
    -1.0925484305920792,
    0.31539156525252005,
    -1.0925484305920792,
    0.5462742152960396,
)
band_three = (
    -0.5900435899266435,
    2.890611442640554,
    -0.4570457994644658,
    0.3731763325901154,
    -0.4570457994644658,
    1.445305721320277,
    -0.5900435899266435,
)
half_log2e = math.sqrt(0.5 * math.log2(math.e))


def params_of(megabytes):
    return pltpu.CompilerParams(vmem_limit_bytes=megabytes << 20)


def harmonics(ray_x, ray_y, ray_z):
    sq_x = ray_x * ray_x
    sq_y = ray_y * ray_y
    sq_z = ray_z * ray_z
    return jnp.stack(
        [
            band_zero * jnp.ones_like(ray_x),
            -band_one * ray_y,
            band_one * ray_z,
            -band_one * ray_x,
            band_two[0] * ray_x * ray_y,
            band_two[1] * ray_y * ray_z,
            band_two[2] * (2.0 * sq_z - sq_x - sq_y),
            band_two[3] * ray_x * ray_z,
            band_two[4] * (sq_x - sq_y),
            band_three[0] * ray_y * (3.0 * sq_x - sq_y),
            band_three[1] * ray_x * ray_y * ray_z,
            band_three[2] * ray_y * (4.0 * sq_z - sq_x - sq_y),
            band_three[3] * ray_z * (2.0 * sq_z - 3.0 * sq_x - 3.0 * sq_y),
            band_three[4] * ray_x * (4.0 * sq_z - sq_x - sq_y),
            band_three[5] * ray_z * (sq_x - sq_y),
            band_three[6] * ray_x * (sq_x - 3.0 * sq_y),
        ]
    )


def project(gauss_rows, camera_row):
    image_width = 1.0 * SIDE * IMG_TX
    image_height = 1.0 * SIDE * IMG_TY
    depth_z = gauss_rows[2]
    screen_u = (gauss_rows[0] - camera_row[0]) / depth_z
    screen_v = (gauss_rows[1] - camera_row[1]) / depth_z
    inv_one = depth_z * depth_z * jnp.exp(-2.0 * gauss_rows[3])
    inv_two = depth_z * depth_z * jnp.exp(-2.0 * gauss_rows[4])
    cosine = jnp.cos(gauss_rows[5])
    sine_angle = jnp.sin(gauss_rows[5])
    conic_a = cosine * cosine * inv_one + sine_angle * sine_angle * inv_two
    conic_b = cosine * sine_angle * (inv_one - inv_two)
    conic_c = sine_angle * sine_angle * inv_one + cosine * cosine * inv_two
    log_opacity = math.log(0.99) - jax.nn.softplus(-gauss_rows[6])
    ray_x = (screen_u - 0.5 * image_width) / image_width
    ray_y = (screen_v - 0.5 * image_height) / image_width
    factor = lax.rsqrt(ray_x * ray_x + ray_y * ray_y + 1.0)
    harmonic_basis = harmonics(ray_x * factor, ray_y * factor, factor)
    coeffs = gauss_rows[7:].reshape(3, NCOEF, gauss_rows.shape[1])
    colour = 0.5 + jnp.sum(coeffs * harmonic_basis[None], axis=1)
    geometry = jnp.stack([screen_u, screen_v, conic_a, conic_b, conic_c, log_opacity])
    return jnp.concatenate([geometry, colour], 0), (inv_one, inv_two)


def factor_rows(projected, inverses):
    conic_a, conic_b, conic_c = projected[2], projected[3], projected[4]
    inv_one, inv_two = inverses
    has_a = conic_a > 0.0
    safe_a = jnp.where(has_a, conic_a, 1.0)
    root = jnp.sqrt(safe_a)
    alpha = jnp.where(has_a, half_log2e * root, 0.0)
    beta = jnp.where(has_a, half_log2e * conic_b / root, 0.0)
    gamma = half_log2e * jnp.where(
        has_a, jnp.sqrt(inv_one * (inv_two / safe_a)), jnp.sqrt(conic_c)
    )
    log2_opacity = jnp.maximum(projected[5] * math.log2(math.e), -1.0e4)
    return jnp.concatenate(
        [projected[0:2], jnp.stack([alpha, beta, gamma, log2_opacity]), projected[6:9]], 0
    )


def split3(values):
    hi = values.astype(BF16).astype(F32)
    rest = values - hi
    mid = rest.astype(BF16).astype(F32)
    return hi, mid, rest - mid


def my_index():
    return lax.axis_index("gx") * lax.axis_size("gy") + lax.axis_index("gy")


def mesh_place(device):
    inner = lax.axis_size("gy")
    return (device // inner, lax.rem(device, inner))


def greet():
    barrier = pltpu.get_barrier_semaphore()
    me = my_index()

    def one(k, _):
        pl.semaphore_signal(
            barrier,
            inc=1,
            device_id=mesh_place(lax.rem(me + k, OWN)),
            device_id_type=pl.DeviceIdType.MESH,
        )
        return 0

    lax.fori_loop(1, OWN, one, 0, unroll=2)


def all_entered():
    pl.semaphore_wait(pltpu.get_barrier_semaphore(), OWN - 1)


def send(source, target, peer, send_sem, recv_sem):
    me = my_index()
    pltpu.make_async_remote_copy(
        src_ref=source.at[:, peer, :],
        dst_ref=target.at[:, me, :],
        send_sem=send_sem,
        recv_sem=recv_sem,
        device_id=mesh_place(peer),
        device_id_type=pl.DeviceIdType.MESH,
    ).start()


def all_but_one(source, target, send_sem, recv_sem):
    blocks = pl.ds(0, OWN - 1)
    return pltpu.make_async_remote_copy(
        src_ref=source.at[:, blocks, :],
        dst_ref=target.at[:, blocks, :],
        send_sem=send_sem,
        recv_sem=recv_sem,
        device_id=mesh_place(my_index()),
        device_id_type=pl.DeviceIdType.MESH,
    )


def keep_own(source, target):
    me = my_index()
    for k in range(source.shape[0]):
        target[k, pl.ds(me, 1), :] = source[k, pl.ds(me, 1), :]


def remote_params(collective_id, megabytes=32):
    return pltpu.CompilerParams(
        collective_id=collective_id, has_side_effects=True, vmem_limit_bytes=megabytes << 20
    )


GROUP = 16


def routing_kernel(ids_ref, tile_ref, upper_ref, slot_ref, asked_ref, request, send_sem, recv_sem):
    greet()
    row_iota = lax.broadcasted_iota(I32, (OWN, LANES), 0)
    own_tile = (lax.broadcasted_iota(I32, (1, LANES), 1) & (TILES_DEV - 1)).astype(F32)
    zero = jnp.zeros((OWN, LANES), BF16)
    upper = upper_ref[...]

    def body(k, carry):
        out = []
        for s in range(STEPS):
            earlier, acc = carry[s]
            members, cells = [], []
            for c in range(GROUP):
                ids = ids_ref[s, pl.ds(k * GROUP + c, 1), :]
                owner = lax.shift_right_logical(ids, 11)
                member = row_iota == owner
                member_bf = jnp.where(member, 1.0, 0.0).astype(BF16)
                ahead = jnp.dot(
                    jnp.concatenate([member_bf, earlier], 1), upper, preferred_element_type=F32
                )
                rank = jnp.sum(
                    jnp.where(member, ahead, 0.0), axis=0, keepdims=True
                ).astype(I32)
                earlier = earlier + member_bf
                slot_ref[s, pl.ds(k * GROUP + c, 1), :] = owner * LANES + rank
                here = row_iota == rank
                low = (ids & 127).astype(F32)
                high = (lax.shift_right_logical(ids, 7) & 15).astype(F32) * 16.0 + own_tile
                members.append(member_bf)
                cells.append(
                    jnp.concatenate(
                        [
                            jnp.where(here, low, 0.0).astype(BF16),
                            jnp.where(here, high, 0.0).astype(BF16),
                        ],
                        0,
                    )
                )
            acc = acc + lax.dot_general(
                jnp.concatenate(members, 1),
                jnp.concatenate(cells, 1),
                (((1,), (1,)), ((), ())),
                preferred_element_type=F32,
            )
            out.append((earlier, acc))
        return tuple(out)

    start = tuple((zero, jnp.zeros((OWN, 2 * LANES), F32)) for _ in range(STEPS))
    done = lax.fori_loop(0, SLABS // GROUP, body, start)
    for s in range(STEPS):
        acc = done[s][1].astype(I32)
        high = acc[:, LANES:]
        request[s] = acc[:, :LANES] + lax.shift_right_logical(high, 4) * 128
        request[STEPS + s] = jnp.take_along_axis(
            jnp.broadcast_to(tile_ref[s], (OWN, LANES)),
            high & 15,
            axis=1,
            mode="promise_in_bounds",
        )
    all_entered()
    me = my_index()

    def push(k, _):
        send(request, asked_ref, lax.rem(me + k, OWN), send_sem, recv_sem)
        return 0

    lax.fori_loop(1, OWN, push, 0, unroll=2)
    keep_own(request, asked_ref)
    rest = all_but_one(request, asked_ref, send_sem, recv_sem)
    rest.wait_send()
    rest.wait_recv()


def routing(ids, lane_tiles):
    strict = np.triu(np.ones((128, 128), np.float32), 1)
    upper = jnp.asarray(np.concatenate([strict, np.ones((128, 128), np.float32)], 0), BF16)
    vmem = pl.BlockSpec(memory_space=pltpu.VMEM)
    return pl.pallas_call(
        routing_kernel,
        out_shape=(
            jax.ShapeDtypeStruct((STEPS, SLABS, LANES), I32),
            jax.ShapeDtypeStruct((2 * STEPS, OWN, LANES), I32),
        ),
        in_specs=[vmem] * 3,
        out_specs=(vmem, vmem),
        scratch_shapes=[
            pltpu.VMEM((2 * STEPS, OWN, LANES), I32),
            pltpu.SemaphoreType.DMA,
            pltpu.SemaphoreType.DMA,
        ],
        compiler_params=remote_params(0),
        name="routing",
    )(ids, lane_tiles, upper)


BLOCKS = 8


def gather_kernel(
    step, table_ref, asked_ref, out_ref, shift_ref, parts, got, answer, send_sem, recv_sem
):
    greet()
    for f in range(FIELDS):
        for p, part in enumerate(split3(table_ref[f])):
            parts[f * 16 : f * 16 + 16, p * 128 : p * 128 + 128] = part.astype(BF16)
    low_iota = lax.broadcasted_iota(I32, (128, 256), 0)
    high_iota = lax.broadcasted_iota(I32, (16, 256), 0)
    me = my_index()
    groups = OWN // BLOCKS

    def group_of(k):
        return lax.rem(me // BLOCKS + k, groups)

    def compute(group):
        first = pl.multiple_of(group * BLOCKS, BLOCKS)
        for pair in range(BLOCKS // 2):
            d = first + 2 * pair
            want = jnp.concatenate(
                [asked_ref[step, pl.ds(d, 1), :], asked_ref[step, pl.ds(d + 1, 1), :]], 1
            )
            hot = jnp.where(low_iota == (want & 127), 1.0, 0.0).astype(BF16)
            hot = jnp.concatenate([hot, hot, hot], 0)
            here = high_iota == lax.shift_right_logical(want, 7)
            picked = jnp.dot(parts[...], hot, preferred_element_type=F32)
            for f in range(FIELDS):
                row = jnp.sum(
                    jnp.where(here, picked[f * 16 : f * 16 + 16], 0.0), axis=0, keepdims=True
                )
                got[f, 2 * pair : 2 * pair + 1, :] = row[:, :128]
                got[f, 2 * pair + 1 : 2 * pair + 2, :] = row[:, 128:]
        at = pl.ds(first, BLOCKS)
        tile = asked_ref[STEPS + step, at, :]
        centre_x = ((tile & (IMG_TX - 1)) * SIDE + SIDE // 2).astype(F32)
        centre_y = (lax.shift_right_logical(tile, 6) * SIDE + SIDE // 2).astype(F32)
        local_u = got[0] - centre_x
        local_v = got[1] - centre_y
        shift_ref[0, at, :] = local_u
        shift_ref[1, at, :] = local_v
        alpha, beta, gamma = got[2], got[3], got[4]
        answer[0, at, :] = alpha
        answer[1, at, :] = beta
        answer[2, at, :] = gamma
        answer[3, at, :] = -(alpha * local_u + beta * local_v)
        answer[4, at, :] = -gamma * local_v
        for f in range(5, FIELDS):
            answer[f, at, :] = got[f]

    def push(group):
        for k in range(BLOCKS):
            peer = group * BLOCKS + lax.rem(me + k, BLOCKS)
            send(answer, out_ref, peer, send_sem, recv_sem)

    def early(k, _):
        compute(group_of(k))
        return 0

    half = groups // 2
    lax.fori_loop(0, half, early, 0)
    all_entered()

    def late(k, _):
        push(group_of(2 * k + 1))
        push(group_of(2 * k + 2))
        compute(group_of(k + half))
        return 0

    lax.fori_loop(0, half - 2, late, 0)
    compute(group_of(groups - 2))
    push(group_of(groups - 3))
    compute(group_of(groups - 1))
    push(group_of(groups - 2))
    push(group_of(groups - 1))

    def inside(k, _):
        send(answer, out_ref, me // BLOCKS * BLOCKS + lax.rem(me + k, BLOCKS), send_sem, recv_sem)
        return 0

    lax.fori_loop(1, BLOCKS, inside, 0)
    keep_own(answer, out_ref)
    rest = all_but_one(answer, out_ref, send_sem, recv_sem)
    rest.wait_send()
    rest.wait_recv()


def owner_gather(step, table, asked):
    vmem = pl.BlockSpec(memory_space=pltpu.VMEM)
    return pl.pallas_call(
        functools.partial(gather_kernel, step),
        out_shape=(
            jax.ShapeDtypeStruct((FIELDS, OWN, LANES), F32),
            jax.ShapeDtypeStruct((2, OWN, LANES), F32),
        ),
        in_specs=[vmem] * 2,
        out_specs=(vmem, vmem),
        scratch_shapes=[
            pltpu.VMEM((FIELDS * 16, 384), BF16),
            pltpu.VMEM((FIELDS, BLOCKS, LANES), F32),
            pltpu.VMEM((FIELDS, OWN, LANES), F32),
            pltpu.SemaphoreType.DMA,
            pltpu.SemaphoreType.DMA,
        ],
        compiler_params=remote_params(1 + step),
        name="owner_gather",
    )(table, asked)


def scatter_kernel(
    step, moment_ref, shift_ref, asked_ref, out_ref, loss_ref,
    arrived, high, rest, own_sem, send_sem, recv_sems,
):
    greet()
    me = my_index()
    groups = OWN // BLOCKS
    mine = me // BLOCKS
    all_entered()

    def push(k, _):
        send(moment_ref, arrived, lax.rem(me + k, OWN), send_sem, recv_sems.at[mine])
        return 0

    lax.fori_loop(1, OWN, push, 0, unroll=2)
    own = pltpu.make_async_copy(moment_ref.at[:, me, :], arrived.at[:, me, :], own_sem)
    own.start()
    own.wait()
    low_iota = lax.broadcasted_iota(I32, (128, 128), 0)
    high_iota = lax.broadcasted_iota(I32, (16, 128), 0)

    def landed(group, count):
        blocks = pl.ds(group * BLOCKS, count)
        pltpu.make_async_remote_copy(
            src_ref=moment_ref.at[:, blocks, :],
            dst_ref=arrived.at[:, blocks, :],
            send_sem=send_sem,
            recv_sem=recv_sems.at[group],
            device_id=mesh_place(me),
            device_id_type=pl.DeviceIdType.MESH,
        ).wait_recv()

    def body(k, carry):
        acc, loss = carry
        group = lax.rem(mine + groups - k, groups)

        @pl.when(k == 0)
        def _():
            landed(group, BLOCKS - 1)

        @pl.when(k != 0)
        def _():
            landed(group, BLOCKS)

        first = pl.multiple_of(group * BLOCKS, BLOCKS)
        at = pl.ds(first, BLOCKS)
        local_u, local_v = shift_ref[0, at, :], shift_ref[1, at, :]
        m0, mx, my = arrived[0, at, :], arrived[1, at, :], arrived[2, at, :]
        sx = mx - local_u * m0
        sy = my - local_v * m0
        sums = [
            sx,
            sy,
            arrived[3, at, :] - local_u * (mx + sx),
            arrived[4, at, :] - local_u * my - local_v * sx,
            arrived[5, at, :] - local_v * (my + sy),
            m0,
            arrived[6, at, :],
            arrived[7, at, :],
            arrived[8, at, :],
        ]
        for f in range(FIELDS):
            top = sums[f].astype(BF16).astype(F32)
            high[f] = top
            rest[f] = sums[f] - top
        for pair in range(BLOCKS // 2):
            lefts, rights = [], []
            for half in range(2):
                d = 2 * pair + half
                want = asked_ref[step, pl.ds(first + d, 1), :]
                rights.append(jnp.where(low_iota == (want & 127), 1.0, 0.0).astype(BF16))
                here = high_iota == lax.shift_right_logical(want, 7)
                rows = [
                    jnp.where(here, ref[f, d : d + 1, :], 0.0).astype(BF16)
                    for ref in (high, rest)
                    for f in range(FIELDS)
                ]
                lefts.append(jnp.concatenate(rows, 0))
            acc = acc + lax.dot_general(
                jnp.concatenate(lefts, 1),
                jnp.concatenate(rights, 1),
                (((1,), (1,)), ((), ())),
                preferred_element_type=F32,
            )
        return acc, loss + arrived[FIELDS, at, :]

    acc, loss = lax.fori_loop(
        0,
        groups,
        body,
        (jnp.zeros((2 * FIELDS * 16, 128), F32), jnp.zeros((BLOCKS, LANES), F32)),
    )
    out_ref[...] = acc[: FIELDS * 16] + acc[FIELDS * 16 :]
    loss_ref[...] = jnp.sum(loss, axis=0, keepdims=True)
    all_but_one(moment_ref, arrived, send_sem, own_sem).wait_send()


def owner_scatter(step, moments, shifts, asked):
    vmem = pl.BlockSpec(memory_space=pltpu.VMEM)
    return pl.pallas_call(
        functools.partial(scatter_kernel, step),
        out_shape=(
            jax.ShapeDtypeStruct((FIELDS * 16, 128), F32),
            jax.ShapeDtypeStruct((1, LANES), F32),
        ),
        in_specs=[vmem] * 3,
        out_specs=(vmem, vmem),
        scratch_shapes=[
            pltpu.VMEM((FIELDS + 1, OWN, LANES), F32),
            pltpu.VMEM((FIELDS, BLOCKS, LANES), F32),
            pltpu.VMEM((FIELDS, BLOCKS, LANES), F32),
            pltpu.SemaphoreType.DMA,
            pltpu.SemaphoreType.DMA,
            pltpu.SemaphoreType.DMA((OWN // BLOCKS,)),
        ],
        compiler_params=remote_params(1 + STEPS + step),
        name="owner_scatter",
    )(moments, shifts, asked)


PACK = 8


def render_constants():
    axis = np.arange(SIDE, dtype=np.float32) - 7.5
    x = np.tile(axis, SIDE)
    y = np.repeat(axis, SIDE)
    one = np.ones_like(x)
    zero = np.zeros_like(x)
    block = np.zeros((8, 512), np.float32)
    block[0] = np.concatenate([x, zero])
    block[1] = np.concatenate([y, zero])
    block[2] = np.concatenate([zero, y])
    block[3] = np.concatenate([one, zero])
    block[4] = np.concatenate([zero, one])
    lines = np.concatenate([block, block, block, np.zeros_like(block)], 0)
    mono = np.zeros((2 * PIX, 128), np.float32)
    for k, column in enumerate((one, x, y, x * x, x * y, y * y)):
        mono[:, k * PACK : (k + 1) * PACK] = np.tile(column, 2)[:, None]
    fold = np.zeros((256, 128), np.float32)
    for ch in range(3):
        for half in range(2):
            at = half * 128 + ch * TILES_DEV
            fold[at : at + TILES_DEV, (6 + ch) * PACK : (7 + ch) * PACK] = 1.0
    return jnp.asarray(lines, BF16), jnp.asarray(mono, BF16), jnp.asarray(fold, BF16)


BATCH = 2
COL_OPACITY = 29


def split2(values):
    high = values.astype(BF16)
    return high, (values - high.astype(F32)).astype(BF16)


def render_kernel(
    slot_ref, fields_ref, target_ref, lines_ref, mono_ref, fold_ref,
    picture_ref, moment_ref,
    table, rows, alphas, weights, out_ref, resid, back,
):
    def build(o, _):
        first = fields_ref[0:8, pl.ds(o, 1), :].reshape(8, LANES)
        last = jnp.broadcast_to(fields_ref[8, pl.ds(o, 1), :], (8, LANES))
        stack = jnp.concatenate([*split3(first), first, last], 0)
        table[pl.ds(pl.multiple_of(o * 128, 128), 128), 0:40] = stack.T
        return 0

    lax.fori_loop(0, OWN, build, 0, unroll=4)

    sublane = lax.broadcasted_iota(I32, (8, LANES), 0)

    def fetch(slab, i):
        source = jnp.minimum(slab, SLABS - 1) * 128 + i * TILES_DEV
        for half in range(0, TILES_DEV, 8):
            got = None
            for t in range(8):
                row = table[pl.ds(slot_ref[source + half + t], 1), :]
                row = jnp.broadcast_to(row, (8, LANES))
                got = row if t == 0 else jnp.where(sublane == t, row, got)
            at = pl.multiple_of(slab * 128, 128) + i * TILES_DEV + half
            rows[pl.ds(at, 8), :] = got

    def forward(slab, state):
        through, red, green, blue = state
        for i in range(8):
            at = pl.ds(pl.multiple_of(slab * 128, 128) + i * 16, 16)
            both = jnp.dot(
                rows[at, 0:32].astype(BF16), lines_ref[...], preferred_element_type=F32
            )
            first = both[:, 0:256]
            second = both[:, 256:512]
            cols = rows[at, COL_OPACITY : COL_OPACITY + 4]
            alpha = jnp.exp2(cols[:, 0:1] - first * first - second * second)
            weight = through * alpha
            through = through - weight
            red = red + weight * cols[:, 1:2]
            green = green + weight * cols[:, 2:3]
            blue = blue + weight * cols[:, 3:4]
            alphas[at, :] = alpha
            weights[at, :] = weight
            back[pl.ds(pl.multiple_of(slab * 256, 256) + i * 32, 32), :] = jnp.zeros(
                (32, LANES), F32
            )
            fetch(slab + 1, i)
        return through, red, green, blue

    for i in range(8):
        fetch(0, i)
    blank = jnp.zeros((TILES_DEV, PIX), F32)
    _, red, green, blue = lax.fori_loop(
        0,
        SLABS,
        forward,
        (jnp.ones((TILES_DEV, PIX), F32), blank, blank, blank),
        unroll=4,
    )
    residuals = []
    total = jnp.zeros((), F32)
    for ch, colour in enumerate((red, green, blue)):
        picture_ref[ch] = colour
        residual = colour - target_ref[ch]
        residuals.append(residual)
        total = total + jnp.sum(residual * residual)
    moment_ref[FIELDS] = jnp.full((OWN, LANES), 0.5 * total, F32)
    res_red, res_green, res_blue = residuals

    padded = jnp.concatenate([*residuals, jnp.zeros((80, PIX), F32)], 0)
    turned = padded.T
    top = turned.astype(BF16)
    resid[:, 0:128] = top
    resid[:, 128:256] = (turned - top.astype(F32)).astype(BF16)

    lane = lax.broadcasted_iota(I32, (128, LANES), 1)
    row = lax.broadcasted_iota(I32, (128, LANES), 0)
    own_tile = (lane & 15) == (row & 15)

    def scatter(slab, i, source, base):
        for t in range(TILES_DEV):
            q = i * TILES_DEV + t
            back[pl.ds(slot_ref[slab * 128 + q], 1), :] = source[base + q : base + q + 1, :]

    own_rows = jnp.concatenate([own_tile] * BATCH, 0)

    def backward(turn, behind, target, previous, source):
        first = pl.multiple_of(turn * (BATCH * 128), BATCH * 128)
        every = pl.ds(first, BATCH * 128)
        weight_top, weight_rest = split2(weights[every, :])
        both = jnp.dot(weight_top, resid[...], preferred_element_type=F32)
        shade = both[:, :128] + both[:, 128:]
        shade = shade + jnp.dot(weight_rest, resid[:, 0:128], preferred_element_type=F32)
        shade = jnp.concatenate(split2(jnp.where(own_rows, shade, 0.0)), 1)
        pieces = [None] * (8 * BATCH)
        for i in range(8 * BATCH - 1, -1, -1):
            at = pl.ds(first + i * 16, 16)
            cols = rows[at, COL_OPACITY : COL_OPACITY + 4]
            gain = (
                res_red * cols[:, 1:2] + res_green * cols[:, 2:3] + res_blue * cols[:, 3:4]
            ) - behind
            pieces[i] = weights[at, :] * gain
            behind = behind + alphas[at, :] * gain
            if source is not None:
                scatter(previous * BATCH + i // 8, i % 8, source, i // 8 * 128)
        slope = jnp.concatenate(split2(jnp.concatenate(pieces, 0)), 1)
        target[...] = jnp.dot(slope, mono_ref[...], preferred_element_type=F32) + jnp.dot(
            shade, fold_ref[...], preferred_element_type=F32
        )
        return behind

    batches = SLABS // BATCH
    outs = [out_ref.at[k] for k in range(2)]
    behind = backward(batches - 1, blank, outs[1], None, None)

    def backward_two(k, behind):
        turn = batches - 2 - 2 * k
        behind = backward(turn, behind, outs[0], turn + 1, outs[1])
        return backward(turn - 1, behind, outs[1], turn, outs[0])

    behind = lax.fori_loop(0, batches // 2 - 1, backward_two, behind)
    backward(0, behind, outs[0], 1, outs[1])
    for i in range(8 * BATCH):
        scatter(i // 8, i % 8, outs[0], i // 8 * 128)

    turn = lax.broadcasted_iota(I32, (128, LANES), 1) & (PACK - 1)
    for g in range(OWN // PACK):
        merged = back[g * 1024 : g * 1024 + 128, :]
        for k in range(1, PACK):
            at = g * 1024 + k * 128
            merged = jnp.where(turn == k, back[at : at + 128, :], merged)
        merged = merged.T
        for f in range(FIELDS):
            moment_ref[f, g * PACK : (g + 1) * PACK, :] = merged[f * PACK : (f + 1) * PACK]


def render(slots, fields, target):
    constants = render_constants()
    vmem = pl.BlockSpec(memory_space=pltpu.VMEM)
    entries = SLABS * 128
    return pl.pallas_call(
        render_kernel,
        out_shape=(
            jax.ShapeDtypeStruct((3, TILES_DEV, PIX), F32),
            jax.ShapeDtypeStruct((FIELDS + 1, OWN, LANES), F32),
        ),
        in_specs=[pl.BlockSpec(memory_space=pltpu.SMEM)] + [vmem] * 5,
        out_specs=(vmem, vmem),
        scratch_shapes=[
            pltpu.VMEM((OWN * LANES, LANES), F32),
            pltpu.VMEM((entries + 256, LANES), F32),
            pltpu.VMEM((entries, PIX), F32),
            pltpu.VMEM((entries, PIX), F32),
            pltpu.VMEM((2, BATCH * 128, LANES), F32),
            pltpu.VMEM((PIX, 256), BF16),
            pltpu.VMEM((OWN * LANES, LANES), F32),
        ],
        compiler_params=params_of(56),
        name="render",
    )(slots, fields, target, *constants)


def adam_update(params, moment_one, second, gradient, step_index):
    step_count = adam_start + step_index + 1
    moment_one = beta_one * moment_one + (1.0 - beta_one) * gradient
    second = beta_two * second + (1.0 - beta_two) * gradient * gradient
    scaled_first = moment_one / (1.0 - beta_one**step_count)
    scaled_second = second / (1.0 - beta_two**step_count)
    params = params - learn_rate * scaled_first / (jnp.sqrt(scaled_second) + adam_eps)
    return (params, moment_one, second)


def per_device(gauss_params, first_moment, second_moment, splat_lists, tile_ids, targets, camera):
    local_count = gauss_params.shape[1]
    params, moment_one, moment_two = (gauss_params, first_moment, second_moment)
    ids = jnp.swapaxes(splat_lists, 1, 2).reshape(STEPS, SLABS, LANES)
    lane_tiles = jnp.tile(tile_ids, (1, LANES // TILES_DEV))
    slots, asked = routing(ids, lane_tiles[:, None, :])
    slots = slots.reshape(STEPS, SLABS * LANES)
    pictures = []
    losses = []
    for step_index in range(STEPS):
        projected, pullback, inverses = jax.vjp(
            lambda values: project(values, camera[step_index]), params, has_aux=True
        )
        table = factor_rows(projected, inverses).reshape(FIELDS, 16, 128)
        fields, shifts = owner_gather(step_index, table, asked)
        target = jnp.swapaxes(targets[step_index], 0, 1)
        picture, moments = render(slots[step_index], fields, target)
        sums, loss = owner_scatter(step_index, moments, shifts, asked)
        sums = sums.reshape(FIELDS, local_count)
        losses.append(loss[0, 0])
        conic_a, conic_b, conic_c = projected[2], projected[3], projected[4]
        cotangent = jnp.concatenate(
            [
                jnp.stack(
                    [
                        conic_a * sums[0] + conic_b * sums[1],
                        conic_b * sums[0] + conic_c * sums[1],
                        -0.5 * sums[2],
                        -sums[3],
                        -0.5 * sums[4],
                    ]
                ),
                sums[5:9],
            ],
            0,
        )
        gradient = pullback(cotangent)[0]
        params, moment_one, moment_two = adam_update(
            params, moment_one, moment_two, gradient, step_index
        )
        pictures.append(jnp.swapaxes(picture, 0, 1))
    loss_values = jnp.stack(losses) / (3.0 * PIX * TILES_DEV * OWN)
    return (params, moment_one, moment_two, jnp.stack(pictures), loss_values)


def solution(mesh):
    both = ("gx", "gy")
    in_specs = (
        P(None, both),
        P(None, both),
        P(None, both),
        P(None, both, None),
        P(None, both),
        P(None, both, None, None),
        P(),
    )
    out_specs = (
        P(None, both),
        P(None, both),
        P(None, both),
        P(None, both, None, None),
        P(),
    )
    return jax.shard_map(
        per_device, mesh=mesh, in_specs=in_specs, out_specs=out_specs, check_vma=False
    )
```
